32 devices in a mesh: dp: 4 (over y, x), expert: 8 (over z, core).
Axes of the slice: x: 2, y: 2, z: 4, core: 2. Of those that a mesh axis runs over, the one named last changes fastest.
Arguments:
- hidden_in: bfloat16 [4096, 2880], P(('dp', 'expert')), may hold values from -6 to 6
- queries: bfloat16 [4096, 4096], P(('dp', 'expert')), may hold values from -50 to 50
- kv_pages: bfloat16 [512, 128, 1024], P(('dp', 'expert')), may hold values from -4.5 to 4.5
- page_table: int32 [128, 4], P(('dp', 'expert')), may hold values from 0 to 15, as said below
- new_rows: int32 [128], P(('dp', 'expert')), may hold values from 1 to 125, as said below
- context: int32 [128], P(('dp', 'expert')), may hold values from 1 to 512, as said below
- sink_logits: float32 [64], replicated, may hold values from 0 to 8
- out_proj: bfloat16 [4096, 2880], P('dp'), may hold values from -0.09375 to 0.09375
- norm_gain: float32 [2880], replicated, may hold values from 0.1 to 1.9
- routes: int32 [4096, 4], P(('dp', 'expert')), may hold values from 0 to 31, all different within a row; in each aligned block of 128 rows (0 to 127, 128 to 255, ...) at most 20 rows name the same one
- route_weights: float32 [4096, 4], P(('dp', 'expert')), may hold values from 0.05 to 1
- gate_up: bfloat16 [32, 2, 2880, 2048], P('expert', None, None, 'dp'), may hold values from -0.109375 to 0.109375
- down_proj: bfloat16 [32, 2048, 2880], P('expert', 'dp'), may hold values from -0.125 to 0.125
Outputs:
- layer_out: bfloat16 [4096, 2880], P(('dp', 'expert'))
The draws below stay inside these ranges and needn't reach their ends.
Inputs may be any that keep to these rules, and one draw needn't show every extreme that they name: `page_table`: each request's table row lists distinct pages of its own block of 16 pages; each block's table holds each of its page numbers once. The new_rows of one block of 4 requests sum to 128; one to three requests of each block have more than one. new_rows <= context; in every block some request has context 4 * 128. Within the 128 rows of one block, no expert is named by more than 20 routes; some expert reaches 20 in every draw.
All inputs are finite; a program needn't handle non-finite values.
Results may differ from the reference program's by a relative error of at most 0.015.
Values may be sent and summed in bfloat16 or wider, within the bound.
No kernel may reach another device: no remote copies, remote signals or barrier semaphores. Data moves between devices by JAX's collectives and lax.ppermute only.
A program may use at most 128 MiB of HBM per device.

```python
import math
import jax
import jax.numpy as jnp
import numpy as np
from jax import lax

D = 2880
QH = 64
KVH = 8
HD = 64
E = 32
TOP = 4
FF = 2048
PAGE = 128
ROWS_DEV = 128
REQ_DEV = 4
PPR = 4
PAGES_DEV = 16
CAP = 20
TOKENS = 4096
REQS = 128
PAGES = 512
N_DP = 4
N_EXPERT = 8


def layout(key):
    base_key = jax.random.fold_in(key, 9137)
    devices = TOKENS // ROWS_DEV
    key_list = jax.random.split(jax.random.fold_in(base_key, 1), devices)
    order = jax.vmap(lambda one_key: jax.random.permutation(one_key, REQ_DEV))(key_list).astype(jnp.int32)
    prefill_count = jax.random.randint(jax.random.fold_in(base_key, 2), (devices, 1), 1, 4).astype(jnp.int32)
    prefill = order < prefill_count
    share_raw = jax.random.randint(jax.random.fold_in(base_key, 3), (devices, REQ_DEV), 1, 100).astype(jnp.int32)
    share_raw = jnp.where(prefill, share_raw, 0)
    prefill_total = ROWS_DEV - (REQ_DEV - prefill_count)
    spare_rows = prefill_total - prefill_count
    share_rows = jnp.where(prefill, 1 + spare_rows * share_raw // jnp.sum(share_raw, axis=1, keepdims=True), 0)
    left_rows = prefill_total - jnp.sum(share_rows, axis=1, keepdims=True)
    share_rows = share_rows + jnp.where(order == 0, left_rows, 0)
    new_rows = jnp.where(prefill, share_rows, 1).astype(jnp.int32)
    max_context = PPR * PAGE
    extra_rows = jax.random.randint(jax.random.fold_in(base_key, 4), (devices, REQ_DEV), 0, max_context + 1).astype(jnp.int32)
    context = jnp.minimum(new_rows + extra_rows, max_context)
    context = jnp.where(order == REQ_DEV - 1, max_context, context).astype(jnp.int32)
    page_keys = jax.random.split(jax.random.fold_in(base_key, 5), devices)
    pages = jax.vmap(lambda one_key: jax.random.permutation(one_key, PAGES_DEV))(page_keys).astype(jnp.int32)
    return (new_rows, context, pages.reshape(devices, REQ_DEV, PPR))


def draw_page_table(key, part):
    new_rows, context, pages = layout(key)
    return pages.reshape(REQS, PPR)


def draw_new_rows(key, part):
    new_rows, context, pages = layout(key)
    return new_rows.reshape(REQS)


def draw_context(key, part):
    new_rows, context, pages = layout(key)
    return context.reshape(REQS)


def draw_kv_pages(key, part):
    shape = (PAGES * PAGE, KVH, HD)
    keys_f = jnp.clip(jax.random.normal(jax.random.fold_in(key, 21), shape, jnp.float32), -4.5, 4.5)
    vals_f = jnp.clip(jax.random.normal(jax.random.fold_in(key, 22), shape, jnp.float32), -4.5, 4.5)
    stacked = jnp.stack([keys_f, vals_f], axis=2)
    return stacked.reshape(PAGES, PAGE, KVH * 2 * HD).astype(jnp.bfloat16)


def draw_queries(key, part):
    devices = TOKENS // ROWS_DEV
    group_size = QH // KVH
    shape = (devices, ROWS_DEV, KVH, group_size, HD)
    query_f = jnp.clip(1.5 * jax.random.normal(jax.random.fold_in(key, 31), shape, jnp.float32), -9.0, 9.0)
    return query_f.reshape(TOKENS, QH * HD).astype(jnp.bfloat16)


def shard_levels(stream_key, shape, shards, least, high):
    loudness, own = 1.0, jax.random.fold_in(stream_key, 6)
    for axis_at, parts in shards:
        draws = jnp.exp(jax.random.uniform(jax.random.fold_in(own, axis_at), (parts,), jnp.float32, least / len(shards), high / len(shards)))
        loudness = loudness * jnp.repeat(draws, shape[axis_at] // parts).reshape([-1 if axis == axis_at else 1 for axis in range(len(shape))])
    return loudness


def assign_block(rng, own, number, rows, amount, top, bound, skew):
    order = jax.random.permutation(rng, amount)
    heavy_load, usual = portions_of(amount, rows * top, bound, skew, True), portions_of(amount, rows * top, bound, skew, False)
    places = jnp.arange(amount)

    def named(lengths, offset_by):
        used = int((lengths > 0).sum())
        fixed = max(1, used // 4)
        passed = fixed + (places - fixed + offset_by * (used - fixed)) % max(1, amount - fixed)
        return jnp.zeros((amount,), jnp.int32).at[order[jnp.where(places < fixed, places, passed)]].set(jnp.asarray(lengths, jnp.int32))

    lengths = jnp.where(number % 4 == 0, named(heavy_load, number // 4), named(usual, number - number // 4 - 1))
    mixed = jax.random.permutation(jax.random.fold_in(own, 3), amount)
    donor, sink = mixed[0:amount // 2 * 2:2], mixed[1:amount // 2 * 2:2]
    slack = jnp.minimum(lengths[donor] - 1, bound - lengths[sink]) // 2
    slack = jnp.where((donor == order[0]) | (sink == order[0]) | (lengths[sink] == 0), 0, jnp.maximum(slack, 0))
    passed = jax.random.randint(jax.random.fold_in(own, 4), (amount // 2,), 0, 1 << 20) % (slack + 1)
    lengths = lengths.at[donor].add(-passed).at[sink].add(passed)
    labels = jnp.searchsorted(jnp.cumsum(lengths), jnp.arange(rows * top), side="right").astype(jnp.int32)
    listing = labels.reshape(top, rows).T
    listing = listing[jax.random.permutation(jax.random.fold_in(own, 1), rows)]
    offset_by = jax.random.randint(jax.random.fold_in(own, 2), (rows, 1), 0, top)
    return jnp.take_along_axis(listing, (jnp.arange(top)[None, :] + offset_by) % top, axis=1)


def portions_of(amount, total, bound, skew, full):
    portions = [(1 << 20) // math.isqrt(standing ** skew) + 1 for standing in range(1, amount + 1)]
    largest = bound if full else min(bound, max(-(-total // amount), total * portions[0] // sum(portions)))
    least = 1 if total - largest >= amount - 1 else 0
    counts, rest = [largest] + [least] * (amount - 1), total - largest - least * (amount - 1)
    while rest > 0:
        free = [i for i in range(1, amount) if counts[i] < largest] or [i for i in range(1, amount) if counts[i] < bound]
        pool, budget = sum([portions[i] for i in free]), rest
        for i in free:
            extra = min(bound - counts[i], max(1, budget * portions[i] // pool), rest)
            counts[i] = counts[i] + extra
            rest = rest - extra
    return np.array(counts)


def normal_values(stream_key, shape, deviation, most, shards=(), held_as=jnp.bfloat16):
    entries = deviation * jax.random.normal(stream_key, shape, jnp.float32)
    if shards:
        entries = entries * shard_levels(stream_key, shape, shards, -0.22, 0.18)
    return jnp.clip(entries, -most, most).astype(held_as)


def setup_inputs(seed: int = 0) -> dict:
    seeds = jax.random.split(jax.random.key(seed), 14)
    hidden_in = normal_values(seeds[0], (TOKENS, D), 1.0, 6.0, ((0, 32),))
    queries = draw_queries(jax.random.fold_in(seeds[13], 71), 0)
    kv_pages = draw_kv_pages(jax.random.fold_in(seeds[13], 71), 0)
    page_table = draw_page_table(jax.random.fold_in(seeds[13], 71), 0)
    new_rows = draw_new_rows(jax.random.fold_in(seeds[13], 71), 0)
    context = draw_context(jax.random.fold_in(seeds[13], 71), 0)
    sink_logits = jnp.clip(jax.random.uniform(seeds[6], (QH,), jnp.float32, 0.0, 8.0), 0.0, 8.0)
    out_proj = normal_values(seeds[7], (QH * HD, D), (QH * HD) ** -0.5, 0.09375, ((0, 4),))
    norm_gain = jnp.clip(1.0 + 0.18 * jax.random.normal(seeds[8], (D,), jnp.float32), 0.1, 1.9)
    routes_keys = jax.random.split(jax.random.fold_in(seeds[9], 1), TOKENS // ROWS_DEV)
    routes_turns = jax.random.permutation(jax.random.fold_in(seeds[9], 3), TOKENS // ROWS_DEV)
    routes = jax.vmap(lambda own, number: assign_block(jax.random.fold_in(seeds[9], 2), own, number, ROWS_DEV, E, TOP, CAP, 1))(routes_keys, routes_turns).reshape((TOKENS, TOP))
    route_weights = jnp.clip(jnp.exp(math.log(1.0) - 2.9957323 * jax.random.uniform(seeds[10], (TOKENS, TOP), jnp.float32) ** shard_levels(seeds[10], (TOKENS, TOP), ((0, 32),), -0.2, 0.2)), 0.05, 1.0)
    gate_up = normal_values(seeds[11], (E, 2, D, FF), D ** -0.5, 0.109375, ((0, 8), (3, 4)))
    down_proj = normal_values(seeds[12], (E, FF, D), FF ** -0.5, 0.125, ((0, 8), (1, 4)))
    return dict(hidden_in=hidden_in, queries=queries, kv_pages=kv_pages, page_table=page_table, new_rows=new_rows, context=context, sink_logits=sink_logits, out_proj=out_proj, norm_gain=norm_gain, routes=routes, route_weights=route_weights, gate_up=gate_up, down_proj=down_proj)


norm_eps = 1e-05

def rounded(value):
    return lax.optimization_barrier(value.astype(jnp.bfloat16)).astype(jnp.float32)

def attend_device(queries, kv_pages, page_table, new_rows, context, sink_logits):
    row_count = queries.shape[0]
    req_count = new_rows.shape[0]
    req_ends = jnp.cumsum(new_rows).astype(jnp.int32)
    row_index = jnp.arange(row_count, dtype=jnp.int32)
    owner_req = lax.optimization_barrier(jnp.sum((row_index[:, None] >= req_ends[None, :]).astype(jnp.int32), axis=1))
    pick_req = (owner_req[:, None] == jnp.arange(req_count, dtype=jnp.int32)[None, :]).astype(jnp.int32)
    position = row_index + lax.optimization_barrier(jnp.sum(pick_req * (context - req_ends)[None, :], axis=1))
    row_pages = lax.optimization_barrier(jnp.sum(pick_req[:, :, None] * page_table[None, :, :], axis=1)).astype(jnp.int32)
    key_span = row_pages.shape[1] * PAGE
    key_pos = jnp.arange(key_span, dtype=jnp.int32)
    visible = key_pos[None, :] <= position[:, None]
    group_size = QH // KVH

    def one_head(head_idx):
        kv_head = lax.dynamic_slice_in_dim(kv_pages, head_idx * 2 * HD, 2 * HD, 2)
        gathered = kv_head[row_pages].reshape(row_count, key_span, 2 * HD)
        key_part = gathered[:, :, :HD].astype(jnp.float32)
        value_part = gathered[:, :, HD:].astype(jnp.float32)
        query_part = lax.dynamic_slice_in_dim(queries, head_idx * group_size * HD, group_size * HD, 1)
        query_part = query_part.reshape(row_count, group_size, HD).astype(jnp.float32)
        sink_part = lax.dynamic_slice_in_dim(sink_logits, head_idx * group_size, group_size, 0)
        scores = jnp.einsum('rgd,rsd->rgs', query_part, key_part) * (1.0 / math.sqrt(HD))
        scores = jnp.where(visible[:, None, :], scores, -jnp.inf)
        row_max = jnp.maximum(lax.optimization_barrier(jnp.max(scores, axis=2)), sink_part[None, :])
        weight = jnp.exp(scores - row_max[:, :, None])
        denom_sum = lax.optimization_barrier(jnp.sum(weight, axis=2)) + jnp.exp(sink_part[None, :] - row_max)
        probs_bf = rounded(weight / denom_sum[:, :, None])
        return jnp.einsum('rgs,rsd->rgd', probs_bf, value_part).astype(jnp.bfloat16)
    head_parts = lax.map(one_head, jnp.arange(KVH, dtype=jnp.int32))
    return jnp.transpose(head_parts, (1, 0, 2, 3)).reshape(row_count, QH * HD)

def reference(hidden_in, queries, kv_pages, page_table, new_rows, context, sink_logits, out_proj, norm_gain, routes, route_weights, gate_up, down_proj):
    devices = N_DP * N_EXPERT

    def per_device(items):
        return attend_device(items[0], items[1], items[2], items[3], items[4], sink_logits)
    attended = lax.map(per_device, (queries.reshape(devices, ROWS_DEV, QH * HD), kv_pages.reshape(devices, PAGES_DEV, PAGE, KVH * 2 * HD), page_table.reshape(devices, REQ_DEV, PPR), new_rows.reshape(devices, REQ_DEV), context.reshape(devices, REQ_DEV)))
    attended = attended.reshape(TOKENS, QH * HD)
    o_out = jnp.dot(attended, out_proj, preferred_element_type=jnp.float32)
    mixed_f = rounded(hidden_in.astype(jnp.float32) + o_out)
    normed = (mixed_f * lax.rsqrt(lax.optimization_barrier(jnp.mean(mixed_f * mixed_f, axis=1, keepdims=True)) + norm_eps) * norm_gain).astype(jnp.bfloat16)
    assign = routes.reshape(devices, ROWS_DEV * TOP)
    onehot = (assign[:, :, None] == jnp.arange(E, dtype=jnp.int32)[None, None, :]).astype(jnp.int32)
    slot_index = lax.optimization_barrier(jnp.sum((jnp.cumsum(onehot, axis=1) - onehot) * onehot, axis=2)).astype(jnp.int32)
    dev_of = jnp.arange(TOKENS * TOP, dtype=jnp.int32) // (ROWS_DEV * TOP)
    flat_rows = jnp.arange(TOKENS * TOP, dtype=jnp.int32) // TOP
    flat_assign = routes.reshape(-1)
    flat_slot = slot_index.reshape(-1)
    row_table = jnp.full((E, devices, CAP), TOKENS, jnp.int32).at[flat_assign, dev_of, flat_slot].set(flat_rows)
    wgt_table = jnp.zeros((E, devices, CAP), jnp.float32).at[flat_assign, dev_of, flat_slot].set(route_weights.reshape(-1))
    padded = jnp.concatenate([normed, jnp.zeros((1, D), jnp.bfloat16)], axis=0)

    def expert_step(carry, item):
        table_e, wgt_e, gate_up_e, down_e = item
        flat_idx = table_e.reshape(-1)
        picked = padded[flat_idx].astype(jnp.float32)
        gate_up_f = jnp.einsum('cd,tdf->tcf', picked, gate_up_e.astype(jnp.float32))
        gate_f = gate_up_f[0]
        up_f = gate_up_f[1]
        hidden = rounded((up_f + 1.0) * gate_f * jax.nn.sigmoid(1.702 * gate_f))
        quarters = hidden.reshape(hidden.shape[0], N_DP, FF // N_DP)
        down_q = down_e.astype(jnp.float32).reshape(N_DP, FF // N_DP, D)
        partials = rounded(jnp.einsum('cqf,qfd->qcd', quarters, down_q))
        expert_out = lax.optimization_barrier(jnp.sum(partials, axis=0))
        carry = carry.at[flat_idx].add(expert_out * wgt_e.reshape(-1)[:, None])
        return (carry, None)
    expert_mix, _ = lax.scan(expert_step, jnp.zeros((TOKENS + 1, D), jnp.float32), (row_table, wgt_table, gate_up, down_proj))
    return (mixed_f + expert_mix[:TOKENS]).astype(jnp.bfloat16)
```

```python
import functools

import jax
import jax.numpy as jnp
from jax import lax
from jax.experimental import pallas as pl
from jax.experimental.pallas import tpu as pltpu
from jax.sharding import Mesh
from jax.sharding import PartitionSpec as P

QH = 64
KVH = 8
HD = 64
E = 32
CAP = 20
GROUP = QH // KVH
TILE = 32
PACK = 4

norm_eps = 1e-05
F32 = jnp.float32
BF16 = jnp.bfloat16


def params(mib, **kw):
    return pltpu.CompilerParams(vmem_limit_bytes=mib << 20, **kw)


def attend_kernel(
    col_s, rows_s, ctx_s, table_s, sink_s, q_ref, kv_ref, o_ref, *, kv_heads, reqs, per_req
):
    page_len = kv_ref.shape[1]
    span = per_req * page_len
    width = 2 * HD
    lane = lax.broadcasted_iota(jnp.int32, (1, width), 1)
    low = lane < HD
    slot = lax.broadcasted_iota(jnp.int32, (1, span), 1)
    row_in = lax.broadcasted_iota(jnp.int32, (TILE, 1), 0)
    head0 = col_s[0] * kv_heads * GROUP

    def one_tile(req, first, last, tile):
        r0 = pl.multiple_of(tile * TILE, TILE)
        row = row_in + r0
        mine = (row >= first) & (row < last)
        limit = jnp.where(mine, row + (ctx_s[req] - last), -1)
        limit = jnp.concatenate([limit] * GROUP, axis=0)
        seen = slot <= limit
        for k in range(kv_heads):
            kv = jnp.concatenate(
                [
                    kv_ref[table_s[req * per_req + p], :, k * width : (k + 1) * width]
                    for p in range(per_req)
                ],
                axis=0,
            )
            parts, sinks = [], []
            for g in range(0, GROUP, 2):
                c0 = (k * GROUP + g) * HD
                pair = q_ref[pl.ds(r0, TILE), c0 : c0 + width].astype(F32) * (HD**-0.5)
                parts.append(jnp.where(low, pair, 0.0).astype(BF16))
                parts.append(jnp.where(low, pltpu.roll(pair, HD, 1), 0.0).astype(BF16))
                for h in (g, g + 1):
                    sinks.append(jnp.full((TILE, 1), sink_s[head0 + k * GROUP + h], F32))
            q = jnp.concatenate(parts, axis=0)
            sink = jnp.concatenate(sinks, axis=0)
            score = lax.dot_general(q, kv, (((1,), (1,)), ((), ())), preferred_element_type=F32)
            score = jnp.where(seen, score, -jnp.inf)
            top = jnp.maximum(jnp.max(score, axis=1, keepdims=True), sink)
            prob = jnp.exp(score - top).astype(BF16)
            ones_v = jnp.where(low, jnp.ones_like(kv), kv)
            both = jnp.dot(prob, ones_v, preferred_element_type=F32)
            swapped = pltpu.roll(both, HD, 1)
            norm = jnp.where(low, both, swapped) + jnp.exp(sink - top)
            out = jnp.where(low, swapped, both) / norm
            for g in range(0, GROUP, 2):
                a = out[g * TILE : (g + 1) * TILE]
                b = out[(g + 1) * TILE : (g + 2) * TILE]
                c0 = (k * GROUP + g) * HD
                old = o_ref[pl.ds(r0, TILE), c0 : c0 + width]
                new = jnp.where(low, a, b).astype(BF16)
                o_ref[pl.ds(r0, TILE), c0 : c0 + width] = jnp.where(mine, new, old)

    def one_req(req, first):
        last = first + rows_s[req]

        def step(tile, carry):
            one_tile(req, first, last, tile)
            return carry

        lax.fori_loop(first // TILE, (last - 1) // TILE + 1, step, 0)
        return last

    lax.fori_loop(0, reqs, one_req, jnp.int32(0))


def attend_group(col, queries, kv_pages, page_table, new_rows, context, sink_logits, groups):
    rows = queries.shape[0]
    pages, page_len, kv_width = kv_pages.shape
    reqs, per_req = page_table.shape
    kv_heads = KVH // groups
    q_width = queries.shape[1] // groups
    body = functools.partial(attend_kernel, kv_heads=kv_heads, reqs=reqs, per_req=per_req)
    flops = 2 * 2 * rows * q_width * per_req * page_len
    return pl.pallas_call(
        body,
        grid_spec=pltpu.PrefetchScalarGridSpec(
            num_scalar_prefetch=5,
            grid=(1,),
            in_specs=[
                pl.BlockSpec((rows, q_width), lambda i, col, *_: (0, col[0])),
                pl.BlockSpec(
                    (pages, page_len, kv_width // groups), lambda i, col, *_: (0, 0, col[0])
                ),
            ],
            out_specs=pl.BlockSpec((rows, q_width), lambda i, *_: (0, 0)),
        ),
        out_shape=jax.ShapeDtypeStruct((rows, q_width), BF16),
        compiler_params=params(32),
        cost_estimate=pl.CostEstimate(
            flops=8 * flops,
            bytes_accessed=2 * (2 * rows * q_width + pages * page_len * kv_width // groups),
            transcendentals=0,
        ),
        name="attend",
    )(col, new_rows, context, page_table.reshape(-1), sink_logits, queries, kv_pages)


def mix_kernel(x_ref, a_ref, b_ref, c_ref, d_ref, gain_ref, mixed_ref, normed_ref):
    total = a_ref[...].astype(F32) + b_ref[...].astype(F32)
    total = total + c_ref[...].astype(F32) + d_ref[...].astype(F32)
    mixed = (x_ref[...].astype(F32) + total).astype(BF16)
    mixed_ref[...] = mixed
    m = mixed.astype(F32)
    scale = lax.rsqrt(jnp.mean(m * m, axis=1, keepdims=True) + norm_eps)
    normed_ref[...] = (m * scale * gain_ref[...]).astype(BF16)


def mix_and_norm(hidden_in, terms, norm_gain):
    rows, width = hidden_in.shape
    block = pl.BlockSpec((rows // 4, width), lambda i: (i, 0))
    return pl.pallas_call(
        mix_kernel,
        grid=(4,),
        in_specs=[block] * 5 + [pl.BlockSpec((1, width), lambda i: (0, 0))],
        out_specs=[block, block],
        out_shape=[jax.ShapeDtypeStruct((rows, width), BF16)] * 2,
        compiler_params=params(32),
        name="mix_norm",
    )(hidden_in, *terms, norm_gain.reshape(1, width))


def pick_kernel(base_s, routes_ref, weights_ref, rows_ref, x_ref, w_ref, *, local):
    rows = routes_ref.shape[2]
    slots = PACK * CAP
    upper = (
        lax.broadcasted_iota(jnp.int32, (rows, rows), 0)
        <= lax.broadcasted_iota(jnp.int32, (rows, rows), 1)
    ).astype(F32).astype(BF16)
    place = lax.broadcasted_iota(jnp.int32, (slots, 1), 0)
    columns, weight = [], 0.0
    for s in range(PACK):
        route = routes_ref[s]
        share = weights_ref[s]
        members, rates = [], []
        for e in range(local):
            hit = route == base_s[0] + e
            members.append(jnp.max(jnp.where(hit, 1.0, 0.0), axis=0, keepdims=True))
            rates.append(jnp.sum(jnp.where(hit, share, 0.0), axis=0, keepdims=True))
        member = jnp.concatenate(members, axis=0)
        counts = jnp.dot(member.astype(BF16), upper, preferred_element_type=F32)
        rank = jnp.where(member > 0.0, counts - 1.0, -1000.0).astype(jnp.int32)
        want = place - s * CAP
        hots = [want == rank[e : e + 1] for e in range(local)]
        weight = weight + jnp.concatenate(
            [
                jnp.sum(jnp.where(hots[e], rates[e], 0.0), axis=1, keepdims=True)
                for e in range(local)
            ],
            axis=0,
        )
        columns.append(
            jnp.concatenate([jnp.where(h, 1.0, 0.0) for h in hots], axis=0).astype(BF16)
        )
    hot = jnp.concatenate(columns, axis=1)
    picked = jnp.dot(hot, rows_ref[...], preferred_element_type=F32).astype(BF16)
    x_ref[...] = picked.reshape(x_ref.shape)
    w_ref[...] = weight.reshape(w_ref.shape)


def pick_rows(base, routes, weights, rows, local):
    senders, top, each = routes.shape
    width = rows.shape[1]
    slots = PACK * CAP
    steps = senders // PACK
    return pl.pallas_call(
        functools.partial(pick_kernel, local=local),
        grid_spec=pltpu.PrefetchScalarGridSpec(
            num_scalar_prefetch=1,
            grid=(steps,),
            in_specs=[
                pl.BlockSpec((PACK, top, each), lambda i, *_: (i, 0, 0)),
                pl.BlockSpec((PACK, top, each), lambda i, *_: (i, 0, 0)),
                pl.BlockSpec((PACK * each, width), lambda i, *_: (i, 0)),
            ],
            out_specs=[
                pl.BlockSpec((local, slots, width), lambda i, *_: (0, i, 0)),
                pl.BlockSpec((local, slots, 1), lambda i, *_: (0, i, 0)),
            ],
        ),
        out_shape=[
            jax.ShapeDtypeStruct((local, senders * CAP, width), BF16),
            jax.ShapeDtypeStruct((local, senders * CAP, 1), F32),
        ],
        compiler_params=params(48),
        cost_estimate=pl.CostEstimate(
            flops=2 * steps * local * slots * PACK * each * width,
            bytes_accessed=2 * (rows.size + local * senders * CAP * width),
            transcendentals=0,
        ),
        name="pick_rows",
    )(base, routes, weights, rows)


def expert_kernel(x_ref, w_ref, up_ref, down_ref, y_ref):
    x = x_ref[0]
    gate = jnp.dot(x, up_ref[0, 0], preferred_element_type=F32)
    up = jnp.dot(x, up_ref[0, 1], preferred_element_type=F32)
    act = ((up + 1.0) * gate * jax.nn.sigmoid(1.702 * gate)).astype(BF16)
    out = jnp.dot(act, down_ref[0], preferred_element_type=F32)
    y_ref[0] = (out * w_ref[0]).astype(BF16)


def run_experts(x, w, gate_up, down_proj, block):
    local, slots, width = x.shape
    units = down_proj.shape[1]
    return pl.pallas_call(
        expert_kernel,
        grid=(local, slots // block),
        in_specs=[
            pl.BlockSpec((1, block, width), lambda e, i: (e, i, 0)),
            pl.BlockSpec((1, block, 1), lambda e, i: (e, i, 0)),
            pl.BlockSpec((1, 2, width, units), lambda e, i: (e, 0, 0, 0)),
            pl.BlockSpec((1, units, width), lambda e, i: (e, 0, 0)),
        ],
        out_specs=pl.BlockSpec((1, block, width), lambda e, i: (e, i, 0)),
        out_shape=jax.ShapeDtypeStruct(x.shape, BF16),
        compiler_params=params(56),
        cost_estimate=pl.CostEstimate(
            flops=2 * 3 * local * slots * width * units,
            bytes_accessed=2 * (2 * x.size + gate_up.size + down_proj.size),
            transcendentals=local * slots * units,
        ),
        name="experts",
    )(x, w, gate_up, down_proj)


def spread_kernel(base_s, routes_ref, y_ref, out_ref, *, local):
    rows = routes_ref.shape[1]
    slots = PACK * CAP
    lower = (
        lax.broadcasted_iota(jnp.int32, (rows, rows), 1)
        <= lax.broadcasted_iota(jnp.int32, (rows, rows), 0)
    ).astype(F32).astype(BF16)
    place = lax.broadcasted_iota(jnp.int32, (1, slots), 1)
    y = y_ref[...].reshape(local * slots, y_ref.shape[2])
    hots = []
    for s in range(PACK):
        route = routes_ref[s]
        want = place - s * CAP
        pieces = []
        for e in range(local):
            hit = jnp.where(route == base_s[0] + e, 1.0, 0.0)
            member = jnp.max(hit, axis=1, keepdims=True)
            wide = jnp.broadcast_to(member, (rows, 128)).astype(BF16)
            counts = jnp.dot(lower, wide, preferred_element_type=F32)[:, :slots]
            rank = jnp.where(member > 0.0, counts - 1.0, -1000.0).astype(jnp.int32)
            pieces.append(jnp.where(rank == want, 1.0, 0.0))
        hots.append(jnp.concatenate(pieces, axis=1).astype(BF16))
    hot = jnp.concatenate(hots, axis=0)
    out_ref[...] = jnp.dot(hot, y, preferred_element_type=F32).astype(BF16)


def spread_rows(base, routes, y):
    senders, each, top = routes.shape
    local, _, width = y.shape
    slots = PACK * CAP
    steps = senders // PACK
    return pl.pallas_call(
        functools.partial(spread_kernel, local=local),
        grid_spec=pltpu.PrefetchScalarGridSpec(
            num_scalar_prefetch=1,
            grid=(steps,),
            in_specs=[
                pl.BlockSpec((PACK, each, top), lambda i, *_: (i, 0, 0)),
                pl.BlockSpec((local, slots, width), lambda i, *_: (0, i, 0)),
            ],
            out_specs=pl.BlockSpec((PACK * each, width), lambda i, *_: (i, 0)),
        ),
        out_shape=jax.ShapeDtypeStruct((senders * each, width), BF16),
        compiler_params=params(48),
        cost_estimate=pl.CostEstimate(
            flops=2 * steps * local * slots * PACK * each * width,
            bytes_accessed=2 * (y.size + senders * each * width),
            transcendentals=0,
        ),
        name="spread_rows",
    )(base, routes, y)


def exchange(value, axes, count, step):
    return lax.ppermute(value, axes, [(i, i ^ step) for i in range(count)])


def attention_and_norm(
    hidden_in, queries, kv_pages, page_table, new_rows, context, sink_logits, out_proj, norm_gain,
    dp, dp_count,
):
    me = lax.axis_index(dp)
    order = list(range(dp_count - 1, 0, -1)) + [0]
    arrived = {}
    for step in order:
        col = (me ^ step).astype(jnp.int32).reshape(1)
        part = attend_group(
            col, queries, kv_pages, page_table, new_rows, context, sink_logits, dp_count
        )
        arrived[step] = exchange(part, dp, dp_count, step) if step else part
    terms = []
    for step in order:
        term = jnp.dot(arrived[step], out_proj, preferred_element_type=F32).astype(BF16)
        terms.append(exchange(term, dp, dp_count, step) if step else term)
    return mix_and_norm(hidden_in, terms, norm_gain)


def layer_gathered(
    hidden_in, queries, kv_pages, page_table, new_rows, context, sink_logits, out_proj, norm_gain,
    routes, route_weights, gate_up, down_proj, *, sizes,
):
    ny, nx, nz, nc = sizes
    everyone = ("y", "x", "z", "core")
    each, top = routes.shape
    local = gate_up.shape[0]
    base = ((lax.axis_index("z") * nc + lax.axis_index("core")) * local).astype(jnp.int32)
    base = base.reshape(1)

    def by_core(info):
        info = lax.all_gather(info, everyone, axis=0, tiled=False)
        info = info.reshape((ny * nx * nz, nc) + info.shape[1:])
        return jnp.swapaxes(info, 0, 1).reshape((ny * nx * nz * nc,) + info.shape[2:])

    all_routes = by_core(routes)
    all_routes_t = jnp.swapaxes(all_routes, 1, 2)
    all_weights_t = jnp.swapaxes(by_core(route_weights), 1, 2)
    mixed, normed = attention_and_norm(
        hidden_in, queries, kv_pages, page_table, new_rows, context, sink_logits, out_proj,
        norm_gain, ("y", "x"), ny * nx,
    )
    rows = lax.all_gather(normed, "z", axis=0, tiled=True)
    rows = lax.all_gather(rows, ("y", "x"), axis=0, tiled=True)
    rows = lax.all_gather(rows, "core", axis=0, tiled=True)
    x, w = pick_rows(base, all_routes_t, all_weights_t, rows, local)
    y = run_experts(x, w, gate_up, down_proj, x.shape[1] // 2)
    total = spread_rows(base, all_routes, y)
    total = lax.psum_scatter(total, "core", scatter_dimension=0, tiled=True)
    total = lax.psum_scatter(total, ("y", "x"), scatter_dimension=0, tiled=True)
    total = lax.psum_scatter(total, "z", scatter_dimension=0, tiled=True)
    return (mixed.astype(F32) + total.astype(F32)).astype(BF16)


def layer_sent(
    hidden_in, queries, kv_pages, page_table, new_rows, context, sink_logits, out_proj, norm_gain,
    routes, route_weights, gate_up, down_proj, *, dp_count,
):
    row_count, model_width = hidden_in.shape
    mixed, normed = attention_and_norm(
        hidden_in, queries, kv_pages, page_table, new_rows, context, sink_logits, out_proj,
        norm_gain, "dp", dp_count,
    )
    assign = routes.reshape(-1)
    onehot = (assign[:, None] == jnp.arange(E, dtype=jnp.int32)[None, :]).astype(jnp.int32)
    slot_index = jnp.sum((jnp.cumsum(onehot, axis=0) - onehot) * onehot, axis=1)
    source = jnp.arange(assign.shape[0], dtype=jnp.int32) // routes.shape[1]
    send_rows = jnp.zeros((E, CAP, model_width), BF16).at[assign, slot_index].set(normed[source])
    copies = jnp.broadcast_to(send_rows[None], (dp_count,) + send_rows.shape)
    copies = copies.reshape(dp_count * E, CAP, model_width)
    everyone = ("dp", "expert")
    blocks = lax.all_to_all(copies, everyone, split_axis=0, concat_axis=0, tiled=True)
    local = gate_up.shape[0]
    shape = blocks.shape
    blocks = blocks.reshape(shape[0] // local, local, CAP, model_width)
    gate_up_f = jnp.einsum("sjcd,jtdf->sjctf", blocks, gate_up, preferred_element_type=F32)
    gate, up = gate_up_f[:, :, :, 0, :], gate_up_f[:, :, :, 1, :]
    hidden = ((up + 1.0) * gate * jax.nn.sigmoid(1.702 * gate)).astype(BF16)
    partials = jnp.einsum("sjcf,jfd->sjcd", hidden, down_proj, preferred_element_type=F32)
    partials = partials.astype(BF16).reshape(shape)
    back = lax.all_to_all(partials, everyone, split_axis=0, concat_axis=0, tiled=True)
    back = jnp.sum(back.reshape(dp_count, E, CAP, model_width).astype(F32), axis=0)
    picked = back[assign, slot_index] * route_weights.reshape(-1)[:, None]
    mix = jnp.sum(picked.reshape(row_count, routes.shape[1], model_width), axis=1)
    return (mixed.astype(F32) + mix).astype(BF16)


def solution(mesh):
    dp_count, expert_count = mesh.shape["dp"], mesh.shape["expert"]
    if dp_count == 4 and expert_count == 8:
        sizes = (2, 2, 4, 2)
        grid = Mesh(mesh.devices.reshape(sizes), ("y", "x", "z", "core"))
        dp, expert, body = ("y", "x"), ("z", "core"), functools.partial(layer_gathered, sizes=sizes)
    else:
        grid = mesh
        dp, expert, body = ("dp",), ("expert",), functools.partial(layer_sent, dp_count=dp_count)
    everyone = dp + expert
    return jax.shard_map(
        body,
        mesh=grid,
        in_specs=(
            P(everyone, None),
            P(everyone, None),
            P(everyone, None, None),
            P(everyone, None),
            P(everyone),
            P(everyone),
            P(),
            P(dp, None),
            P(),
            P(everyone, None),
            P(everyone, None),
            P(expert, None, None, dp),
            P(expert, dp, None),
        ),
        out_specs=P(everyone, None),
        check_vma=False,
    )
```

```python
import functools

import jax
import jax.numpy as jnp
from jax import lax
from jax.experimental import pallas as pl
from jax.experimental.pallas import tpu as pltpu
from jax.sharding import Mesh
from jax.sharding import PartitionSpec as P

QH = 64
KVH = 8
HD = 64
E = 32
CAP = 20
GROUP = QH // KVH
TILE = 32
VMEM_MIB = 58

norm_eps = 1e-05
F32 = jnp.float32
BF16 = jnp.bfloat16


def params(mib, **kw):
    return pltpu.CompilerParams(vmem_limit_bytes=mib << 20, **kw)


def attend_kernel(
    col_s, rows_s, ctx_s, table_s, sink_s, q_ref, kv_ref, o_ref, *, kv_heads, reqs, per_req
):
    page_len = kv_ref.shape[1]
    span = per_req * page_len
    width = 2 * HD
    lane = lax.broadcasted_iota(jnp.int32, (1, width), 1)
    low = lane < HD
    slot = lax.broadcasted_iota(jnp.int32, (1, span), 1)
    row_in = lax.broadcasted_iota(jnp.int32, (TILE, 1), 0)
    head0 = col_s[0] * kv_heads * GROUP

    def one_tile(req, first, last, tile):
        r0 = pl.multiple_of(tile * TILE, TILE)
        row = row_in + r0
        mine = (row >= first) & (row < last)
        limit = jnp.where(mine, row + (ctx_s[req] - last), -1)
        limit = jnp.concatenate([limit] * GROUP, axis=0)
        seen = slot <= limit
        for k in range(kv_heads):
            kv = jnp.concatenate(
                [
                    kv_ref[table_s[req * per_req + p], :, k * width : (k + 1) * width]
                    for p in range(per_req)
                ],
                axis=0,
            )
            parts, sinks = [], []
            for g in range(0, GROUP, 2):
                c0 = (k * GROUP + g) * HD
                pair = q_ref[pl.ds(r0, TILE), c0 : c0 + width].astype(F32) * (HD**-0.5)
                parts.append(jnp.where(low, pair, 0.0).astype(BF16))
                parts.append(jnp.where(low, pltpu.roll(pair, HD, 1), 0.0).astype(BF16))
                for h in (g, g + 1):
                    sinks.append(jnp.full((TILE, 1), sink_s[head0 + k * GROUP + h], F32))
            q = jnp.concatenate(parts, axis=0)
            sink = jnp.concatenate(sinks, axis=0)
            score = lax.dot_general(q, kv, (((1,), (1,)), ((), ())), preferred_element_type=F32)
            score = jnp.where(seen, score, -jnp.inf)
            top = jnp.maximum(jnp.max(score, axis=1, keepdims=True), sink)
            prob = jnp.exp(score - top).astype(BF16)
            ones_v = jnp.where(low, jnp.ones_like(kv), kv)
            both = jnp.dot(prob, ones_v, preferred_element_type=F32)
            swapped = pltpu.roll(both, HD, 1)
            norm = jnp.where(low, both, swapped) + jnp.exp(sink - top)
            out = jnp.where(low, swapped, both) / norm
            for g in range(0, GROUP, 2):
                a = out[g * TILE : (g + 1) * TILE]
                b = out[(g + 1) * TILE : (g + 2) * TILE]
                c0 = (k * GROUP + g) * HD
                old = o_ref[pl.ds(r0, TILE), c0 : c0 + width]
                new = jnp.where(low, a, b).astype(BF16)
                o_ref[pl.ds(r0, TILE), c0 : c0 + width] = jnp.where(mine, new, old)

    def one_req(req, first):
        last = first + rows_s[req]

        def step(tile, carry):
            one_tile(req, first, last, tile)
            return carry

        lax.fori_loop(first // TILE, (last - 1) // TILE + 1, step, 0)
        return last

    lax.fori_loop(0, reqs, one_req, jnp.int32(0))


def attend_group(col, queries, kv_pages, page_table, new_rows, context, sink_logits, groups):
    rows = queries.shape[0]
    pages, page_len, kv_width = kv_pages.shape
    reqs, per_req = page_table.shape
    kv_heads = KVH // groups
    q_width = queries.shape[1] // groups
    body = functools.partial(attend_kernel, kv_heads=kv_heads, reqs=reqs, per_req=per_req)
    flops = 2 * 2 * rows * q_width * per_req * page_len
    return pl.pallas_call(
        body,
        grid_spec=pltpu.PrefetchScalarGridSpec(
            num_scalar_prefetch=5,
            grid=(1,),
            in_specs=[
                pl.BlockSpec((rows, q_width), lambda i, col, *_: (0, col[0])),
                pl.BlockSpec(
                    (pages, page_len, kv_width // groups), lambda i, col, *_: (0, 0, col[0])
                ),
            ],
            out_specs=pl.BlockSpec((rows, q_width), lambda i, *_: (0, 0)),
        ),
        out_shape=jax.ShapeDtypeStruct((rows, q_width), BF16),
        compiler_params=params(VMEM_MIB),
        cost_estimate=pl.CostEstimate(
            flops=8 * flops,
            bytes_accessed=2 * (2 * rows * q_width + pages * page_len * kv_width // groups),
            transcendentals=0,
        ),
        name="attend",
    )(col, new_rows, context, page_table.reshape(-1), sink_logits, queries, kv_pages)


def mix_kernel(x_ref, a_ref, b_ref, c_ref, d_ref, gain_ref, mixed_ref, normed_ref):
    total = a_ref[...].astype(F32) + b_ref[...].astype(F32)
    total = total + c_ref[...].astype(F32) + d_ref[...].astype(F32)
    mixed = (x_ref[...].astype(F32) + total).astype(BF16)
    mixed_ref[...] = mixed
    m = mixed.astype(F32)
    scale = lax.rsqrt(jnp.mean(m * m, axis=0, keepdims=True) + norm_eps)
    normed = (jnp.transpose(m * scale) * gain_ref[...]).astype(BF16)
    rows, width = normed.shape
    normed_ref[:, :width] = normed
    if normed_ref.shape[1] > width:
        normed_ref[:, width:] = jnp.zeros((rows, normed_ref.shape[1] - width), BF16)


def mix_and_norm(hidden_t, terms_t, norm_gain):
    width, rows = hidden_t.shape
    normed = jax.ShapeDtypeStruct((rows, -(-width // 128) * 128), BF16)
    return pl.pallas_call(
        mix_kernel,
        out_shape=[jax.ShapeDtypeStruct((width, rows), BF16), normed],
        compiler_params=params(VMEM_MIB),
        name="mix_norm",
    )(hidden_t, *terms_t, norm_gain.reshape(1, width))


def finish_kernel(mixed_ref, *refs):
    parts, out_ref = refs[:-1], refs[-1]
    total = parts[0][...].astype(F32)
    for part in parts[1:]:
        total = total + part[...].astype(F32)
    total = jnp.transpose(total)[: mixed_ref.shape[0]]
    out_ref[...] = (mixed_ref[...].astype(F32) + total).astype(BF16)


def finish(mixed_t, parts):
    return pl.pallas_call(
        finish_kernel,
        out_shape=jax.ShapeDtypeStruct(mixed_t.shape, BF16),
        compiler_params=params(VMEM_MIB),
        name="finish",
    )(mixed_t, *parts)


def back_order():
    return [3, 1, 2, 0]


def pick_plane(base, info_ref, plane, rows, x_ref, w_ref, hot_ref, *, local, count):
    each = info_ref.shape[2]
    top = info_ref.shape[1] // 2
    slots = count * CAP
    upper = (
        lax.broadcasted_iota(jnp.int32, (each, each), 0)
        <= lax.broadcasted_iota(jnp.int32, (each, each), 1)
    ).astype(F32).astype(BF16)
    place = lax.broadcasted_iota(jnp.int32, (slots, 1), 0)
    columns, weight = [], 0.0
    for s in range(count):
        info = info_ref[plane * count + s]
        route, share = info[:top], info[top:]
        members, rates = [], []
        for e in range(local):
            hit = route == (base + e).astype(F32)
            members.append(jnp.max(jnp.where(hit, 1.0, 0.0), axis=0, keepdims=True))
            rates.append(jnp.sum(jnp.where(hit, share, 0.0), axis=0, keepdims=True))
        member = jnp.concatenate(members, axis=0)
        counts = jnp.dot(member.astype(BF16), upper, preferred_element_type=F32)
        rank = jnp.where(member > 0.0, counts - 1.0, -1000.0).astype(jnp.int32)
        want = place - s * CAP
        hots = [want == rank[e : e + 1] for e in range(local)]
        weight = weight + jnp.concatenate(
            [
                jnp.sum(jnp.where(hots[e], rates[e], 0.0), axis=1, keepdims=True)
                for e in range(local)
            ],
            axis=0,
        )
        columns.append(jnp.concatenate([jnp.where(h, 1.0, 0.0) for h in hots], axis=0))
    for i, s in enumerate(back_order()):
        hot_ref[plane, i * each : (i + 1) * each, :] = jnp.transpose(columns[s]).astype(BF16)
    hot = jnp.concatenate([c.astype(BF16) for c in columns], axis=1)
    picked = jnp.dot(hot, rows, preferred_element_type=F32).astype(BF16)[:, : x_ref.shape[2]]
    for e in range(local):
        x_ref[e, plane * slots : (plane + 1) * slots, :] = picked[e * slots : (e + 1) * slots]
        w_ref[e, plane * slots : (plane + 1) * slots, :] = jnp.broadcast_to(
            weight[e * slots : (e + 1) * slots], (slots, 128)
        )


def chunk_kernel(
    base_s, info_ref, *refs, local, count, splits, held, passed,
):
    pieces, refs = refs[:held], refs[held:]
    up_ref, down_ref, refs = refs[0], refs[1], refs[2 + passed :]
    mine_out, far_out, other_out, refs = refs[0], refs[1], refs[2], refs[3 + passed :]
    x_ref, w_ref, hot_ref, acc_ref, y_ref = refs
    step = pl.program_id(0)
    e = step // splits
    part_at = step % splits
    slots = count * CAP

    @pl.when(step == 0)
    def _():
        for plane in (0, 1):
            rows = [ref[...] for ref in pieces[plane * held // 2 : (plane + 1) * held // 2]]
            rows = jnp.concatenate(rows, axis=0)
            pick_plane(
                base_s[0], info_ref, plane, rows, x_ref, w_ref, hot_ref,
                local=local, count=count,
            )

    x = x_ref[e]
    gate = jnp.dot(x, up_ref[0, 0], preferred_element_type=F32)
    up = jnp.dot(x, up_ref[0, 1], preferred_element_type=F32)
    act = ((up + 1.0) * gate * jax.nn.sigmoid(1.702 * gate)).astype(BF16)
    part = lax.dot_general(
        act, down_ref[0], (((1,), (1,)), ((), ())), preferred_element_type=F32
    )

    @pl.when(part_at == 0)
    def _():
        acc_ref[...] = part

    @pl.when(part_at > 0)
    def _():
        acc_ref[...] += part

    @pl.when(part_at == splits - 1)
    def _():
        y = (acc_ref[...] * w_ref[e][:, :1]).astype(BF16)
        at = pl.ds(pl.multiple_of(e * slots, 16), slots)
        for plane in (0, 1):
            y_ref[plane, at, :] = y[plane * slots : (plane + 1) * slots]

    @pl.when(step == local * splits - 1)
    def _():
        far = far_out.shape[0]
        for plane, refs_at in enumerate(([(mine_out, 0)], [(far_out, 0), (other_out, far)])):
            total = jnp.dot(hot_ref[plane], y_ref[plane], preferred_element_type=F32).astype(BF16)
            width = total.shape[1]
            for ref, at in refs_at:
                ref[:, :width] = total[at : at + ref.shape[0]]
                if ref.shape[1] > width:
                    fill = (ref.shape[0], ref.shape[1] - width)
                    ref[:, width:] = jnp.zeros(fill, BF16)


def run_chunk(base, info, pieces, gate_up, down_t, later=()):
    senders, fields, each = info.shape
    count = senders // 2
    local, _, width, units = gate_up.shape
    splits = 2
    slots = count * CAP
    unit = units // splits
    wide = pieces[0].shape[1]
    whole = [pl.BlockSpec(p.shape, lambda i, *_: (0, 0)) for p in pieces]
    heights = [count * each, each, (count - 1) * each]
    macs = 2 * local * slots * width * (3 * units + 2 * count * each)
    body = functools.partial(
        chunk_kernel, local=local, count=count, splits=splits, held=len(pieces), passed=len(later)
    )
    hand_on = [pl.BlockSpec(memory_space=pl.ANY)] * len(later)
    first_later = 4 + len(pieces)
    return pl.pallas_call(
        body,
        grid_spec=pltpu.PrefetchScalarGridSpec(
            num_scalar_prefetch=1,
            grid=(local * splits,),
            in_specs=[
                pl.BlockSpec((senders, fields, each), lambda i, *_: (0, 0, 0)),
                *whole,
                pl.BlockSpec((1, 2, width, unit), lambda i, *_: (i // splits, 0, 0, i % splits)),
                pl.BlockSpec((1, width, unit), lambda i, *_: (i // splits, 0, i % splits)),
                *hand_on,
            ],
            out_specs=[
                *[pl.BlockSpec((h, wide), lambda i, *_: (0, 0)) for h in heights],
                *hand_on,
            ],
            scratch_shapes=[
                pltpu.VMEM((local, 2 * slots, width), BF16),
                pltpu.VMEM((local, 2 * slots, 128), F32),
                pltpu.VMEM((2, count * each, local * slots), BF16),
                pltpu.VMEM((2 * slots, width), F32),
                pltpu.VMEM((2, local * slots, width), BF16),
            ],
        ),
        out_shape=[
            *[jax.ShapeDtypeStruct((h, wide), BF16) for h in heights],
            *[jax.ShapeDtypeStruct(p.shape, p.dtype) for p in later],
        ],
        input_output_aliases={first_later + i: 3 + i for i in range(len(later))},
        compiler_params=params(VMEM_MIB),
        cost_estimate=pl.CostEstimate(
            flops=2 * macs,
            bytes_accessed=2 * (gate_up.size + down_t.size + 4 * count * each * wide),
            transcendentals=0,
        ),
        name="chunk",
    )(base, info, *pieces, gate_up, down_t, *later)


def exchange(value, axes, count, step):
    return lax.ppermute(value, axes, [(i, i ^ step) for i in range(count)])


def add(a, b):
    return (a.astype(F32) + b.astype(F32)).astype(BF16)


def attention_and_norm(
    hidden_in, queries, kv_pages, page_table, new_rows, context, sink_logits, out_proj, norm_gain,
    dp, dp_count,
):
    me = lax.axis_index(dp)
    order = list(range(dp_count - 1, 0, -1)) + [0]
    arrived = {}
    for step in order:
        col = (me ^ step).astype(jnp.int32).reshape(1)
        part = attend_group(
            col, queries, kv_pages, page_table, new_rows, context, sink_logits, dp_count
        )
        arrived[step] = exchange(part, dp, dp_count, step) if step else part
    terms = []
    for step in order:
        term = jnp.dot(arrived[step], out_proj, preferred_element_type=F32).astype(BF16)
        term = jnp.swapaxes(term, 0, 1)
        terms.append(exchange(term, dp, dp_count, step) if step else term)
    return mix_and_norm(jnp.swapaxes(hidden_in, 0, 1), terms, norm_gain)


def second_hop(mine, other, a_xy, b_xy, to):
    half = a_xy.shape[0]
    each = 2 * half
    for_x = add(mine[each : 2 * each], other[:each])
    for_y = add(mine[2 * each : 3 * each], other[each : 2 * each])
    for_x = jnp.concatenate([add(for_x[:half], a_xy), for_x[half:]], axis=0)
    for_y = jnp.concatenate([for_y[:half], add(for_y[half:], b_xy)], axis=0)
    return to(for_x, "x"), to(for_y, "y")


def layer_gathered(
    hidden_in, queries, kv_pages, page_table, new_rows, context, sink_logits, out_proj, norm_gain,
    routes, route_weights, gate_up, down_proj, *, sizes,
):
    ny, nx, nz, nc = sizes
    local = gate_up.shape[0]
    half = hidden_in.shape[0] // 2
    base = ((lax.axis_index("z") * nc + lax.axis_index("core")) * local).astype(jnp.int32)
    base = base.reshape(1)

    def to(value, axis, step=1):
        return exchange(value, axis, nz if axis == "z" else 2, step)

    info = jnp.concatenate([routes.astype(F32), route_weights], axis=1)
    info = jnp.swapaxes(info, 0, 1)[None]
    for axis, step in (("x", 1), ("y", 1), ("core", 1), ("z", 1), ("z", 2)):
        info = jnp.concatenate([info, to(info, axis, step)], axis=0)
    info = info.reshape((nz, ny * nx * nc) + info.shape[1:])

    mixed, normed = attention_and_norm(
        hidden_in, queries, kv_pages, page_table, new_rows, context, sink_logits, out_proj,
        norm_gain, ("y", "x"), ny * nx,
    )
    down_t = jnp.swapaxes(down_proj, 1, 2)
    rows = {0: normed, 1: to(normed, "z", 1), 2: to(normed, "z", 2)}
    rows[3] = to(rows[2], "z", 1)
    each = 2 * half
    order = (0, 2, 3, 1)
    sums, held, came = {}, {}, {}
    for at, r in enumerate(order):
        own = rows[r]
        own_x, own_y = to(own, "x"), to(own, "y")
        pieces = [own, own_x, own_y, to(own_x[:half], "y"), to(own_y[half:], "x")]
        pieces += [to(piece, "core") for piece in pieces]
        later = {("row", n): rows[n] for n in order[at + 2 : at + 3]}
        later.update({("far", n): held[n][2:] for n in order[at - 2 : at - 1] if at > 1})
        flat, tree = jax.tree.flatten(later)
        mine, far, other, *flat = run_chunk(base, info[r], pieces, gate_up, down_t, flat)
        later = jax.tree.unflatten(tree, flat)
        for (what, n), value in later.items():
            if what == "row":
                rows[n] = value
            elif what == "far":
                came[n] = second_hop(held[n][0], held[n][1], *value, to)
            else:
                came[n] = value
        far, other = to(far, "core"), to(other, "core")
        far = add(mine[:each], far)
        held[r] = (mine, other, to(far[:half], "y"), to(far[half:], "x"))
    for r in order[2:]:
        came[r] = second_hop(*held[r], to)
    for r in order:
        mine, other = held[r][:2]
        kept = add(mine[3 * each :], other[2 * each :])
        sums[r] = add(add(kept, came[r][0]), came[r][1])
        if r:
            sums[r] = to(sums[r], "z", r)
    return jnp.swapaxes(finish(mixed, [sums[r] for r in range(nz)]), 0, 1)


def layer_sent(
    hidden_in, queries, kv_pages, page_table, new_rows, context, sink_logits, out_proj, norm_gain,
    routes, route_weights, gate_up, down_proj, *, dp_count,
):
    row_count, model_width = hidden_in.shape
    mixed, normed = attention_and_norm(
        hidden_in, queries, kv_pages, page_table, new_rows, context, sink_logits, out_proj,
        norm_gain, "dp", dp_count,
    )
    mixed = jnp.swapaxes(mixed, 0, 1)
    normed = normed[:, :model_width]
    assign = routes.reshape(-1)
    onehot = (assign[:, None] == jnp.arange(E, dtype=jnp.int32)[None, :]).astype(jnp.int32)
    slot_index = jnp.sum((jnp.cumsum(onehot, axis=0) - onehot) * onehot, axis=1)
    source = jnp.arange(assign.shape[0], dtype=jnp.int32) // routes.shape[1]
    send_rows = jnp.zeros((E, CAP, model_width), BF16).at[assign, slot_index].set(normed[source])
    copies = jnp.broadcast_to(send_rows[None], (dp_count,) + send_rows.shape)
    copies = copies.reshape(dp_count * E, CAP, model_width)
    everyone = ("dp", "expert")
    blocks = lax.all_to_all(copies, everyone, split_axis=0, concat_axis=0, tiled=True)
    local = gate_up.shape[0]
    shape = blocks.shape
    blocks = blocks.reshape(shape[0] // local, local, CAP, model_width)
    gate_up_f = jnp.einsum("sjcd,jtdf->sjctf", blocks, gate_up, preferred_element_type=F32)
    gate, up = gate_up_f[:, :, :, 0, :], gate_up_f[:, :, :, 1, :]
    hidden = ((up + 1.0) * gate * jax.nn.sigmoid(1.702 * gate)).astype(BF16)
    partials = jnp.einsum("sjcf,jfd->sjcd", hidden, down_proj, preferred_element_type=F32)
    partials = partials.astype(BF16).reshape(shape)
    back = lax.all_to_all(partials, everyone, split_axis=0, concat_axis=0, tiled=True)
    back = jnp.sum(back.reshape(dp_count, E, CAP, model_width).astype(F32), axis=0)
    picked = back[assign, slot_index] * route_weights.reshape(-1)[:, None]
    mix = jnp.sum(picked.reshape(row_count, routes.shape[1], model_width), axis=1)
    return (mixed.astype(F32) + mix).astype(BF16)


def solution(mesh):
    dp_count, expert_count = mesh.shape["dp"], mesh.shape["expert"]
    if dp_count == 4 and expert_count == 8:
        sizes = (2, 2, 4, 2)
        grid = Mesh(mesh.devices.reshape(sizes), ("y", "x", "z", "core"))
        dp, expert, body = ("y", "x"), ("z", "core"), functools.partial(layer_gathered, sizes=sizes)
    else:
        grid = mesh
        dp, expert, body = ("dp",), ("expert",), functools.partial(layer_sent, dp_count=dp_count)
    everyone = dp + expert
    return jax.shard_map(
        body,
        mesh=grid,
        in_specs=(
            P(everyone, None),
            P(everyone, None),
            P(everyone, None, None),
            P(everyone, None),
            P(everyone),
            P(everyone),
            P(),
            P(dp, None),
            P(),
            P(everyone, None),
            P(everyone, None),
            P(expert, None, None, dp),
            P(expert, dp, None),
        ),
        out_specs=P(everyone, None),
        check_vma=False,
    )
```

```python
import functools

import jax
import jax.numpy as jnp
from jax import lax
from jax.experimental import pallas as pl
from jax.experimental.pallas import tpu as pltpu
from jax.sharding import Mesh
from jax.sharding import PartitionSpec as P

QH = 64
KVH = 8
HD = 64
E = 32
CAP = 20
BACK = (2, 3, 0, 1)
GROUP = QH // KVH
TILE = 32
VMEM_MIB = 58

norm_eps = 1e-05
F32 = jnp.float32
BF16 = jnp.bfloat16


def params(mib, **kw):
    return pltpu.CompilerParams(vmem_limit_bytes=mib << 20, **kw)


def attend_kernel(
    col_s, rows_s, ctx_s, table_s, sink_s, q_ref, kv_ref, *refs, kv_heads, reqs, per_req
):
    o_ref = refs[-1]
    page_len = kv_ref.shape[1]
    span = per_req * page_len
    width = 2 * HD
    lane = lax.broadcasted_iota(jnp.int32, (1, width), 1)
    low = lane < HD
    slot = lax.broadcasted_iota(jnp.int32, (1, span), 1)
    row_in = lax.broadcasted_iota(jnp.int32, (TILE, 1), 0)
    head0 = (col_s[0] * pl.num_programs(0) + pl.program_id(0)) * kv_heads * GROUP

    def one_tile(req, first, last, tile):
        r0 = pl.multiple_of(tile * TILE, TILE)
        row = row_in + r0
        mine = (row >= first) & (row < last)
        limit = jnp.where(mine, row + (ctx_s[req] - last), -1)
        limit = jnp.concatenate([limit] * GROUP, axis=0)
        seen = slot <= limit
        for k in range(kv_heads):
            kv = jnp.concatenate(
                [
                    kv_ref[table_s[req * per_req + p], :, k * width : (k + 1) * width]
                    for p in range(per_req)
                ],
                axis=0,
            )
            parts, sinks = [], []
            for g in range(0, GROUP, 2):
                c0 = (k * GROUP + g) * HD
                pair = q_ref[pl.ds(r0, TILE), c0 : c0 + width].astype(F32) * (HD**-0.5)
                parts.append(jnp.where(low, pair, 0.0).astype(BF16))
                parts.append(jnp.where(low, pltpu.roll(pair, HD, 1), 0.0).astype(BF16))
                for h in (g, g + 1):
                    sinks.append(jnp.full((TILE, 1), sink_s[head0 + k * GROUP + h], F32))
            q = jnp.concatenate(parts, axis=0)
            sink = jnp.concatenate(sinks, axis=0)
            score = lax.dot_general(q, kv, (((1,), (1,)), ((), ())), preferred_element_type=F32)
            score = jnp.where(seen, score, -jnp.inf)
            top = jnp.maximum(jnp.max(score, axis=1, keepdims=True), sink)
            prob = jnp.exp(score - top).astype(BF16)
            ones_v = jnp.where(low, jnp.ones_like(kv), kv)
            both = jnp.dot(prob, ones_v, preferred_element_type=F32)
            swapped = pltpu.roll(both, HD, 1)
            norm = jnp.where(low, both, swapped) + jnp.exp(sink - top)
            out = jnp.where(low, swapped, both) / norm
            for g in range(0, GROUP, 2):
                a = out[g * TILE : (g + 1) * TILE]
                b = out[(g + 1) * TILE : (g + 2) * TILE]
                c0 = (k * GROUP + g) * HD
                old = o_ref[pl.ds(r0, TILE), c0 : c0 + width]
                new = jnp.where(low, a, b).astype(BF16)
                o_ref[pl.ds(r0, TILE), c0 : c0 + width] = jnp.where(mine, new, old)

    def one_req(req, first):
        last = first + rows_s[req]

        def step(tile, carry):
            one_tile(req, first, last, tile)
            return carry

        lax.fori_loop(first // TILE, (last - 1) // TILE + 1, step, 0)
        return last

    lax.fori_loop(0, reqs, one_req, jnp.int32(0))


def attend_group(
    col, queries, kv_pages, page_table, new_rows, context, sink_logits, groups, before=()
):
    rows = queries.shape[0]
    pages, page_len, kv_width = kv_pages.shape
    reqs, per_req = page_table.shape
    steps = KVH // groups
    q_width = queries.shape[1] // groups
    body = functools.partial(attend_kernel, kv_heads=1, reqs=reqs, per_req=per_req)
    flops = 2 * 2 * rows * q_width * per_req * page_len
    return pl.pallas_call(
        body,
        grid_spec=pltpu.PrefetchScalarGridSpec(
            num_scalar_prefetch=5,
            grid=(steps,),
            in_specs=[
                pl.BlockSpec((rows, q_width // steps), lambda i, col, *_: (0, col[0] * steps + i)),
                pl.BlockSpec(
                    (pages, page_len, kv_width // KVH),
                    lambda i, col, *_: (0, 0, col[0] * steps + i),
                ),
                *[pl.BlockSpec(memory_space=pl.ANY)] * len(before),
            ],
            out_specs=pl.BlockSpec((rows, q_width // steps), lambda i, *_: (0, i)),
        ),
        out_shape=jax.ShapeDtypeStruct((rows, q_width), BF16),
        compiler_params=params(VMEM_MIB),
        cost_estimate=pl.CostEstimate(
            flops=8 * flops,
            bytes_accessed=2 * (2 * rows * q_width + pages * page_len * kv_width // groups),
            transcendentals=0,
        ),
        name="attend",
    )(col, new_rows, context, page_table.reshape(-1), sink_logits, queries, kv_pages, *before)


def mix_kernel(x_ref, a_ref, b_ref, c_ref, d_ref, gain_ref, mixed_ref, normed_ref):
    total = a_ref[...].astype(F32) + b_ref[...].astype(F32)
    total = total + c_ref[...].astype(F32) + d_ref[...].astype(F32)
    mixed = (x_ref[...].astype(F32) + total).astype(BF16)
    mixed_ref[...] = mixed
    m = mixed.astype(F32)
    scale = lax.rsqrt(jnp.mean(m * m, axis=0, keepdims=True) + norm_eps)
    normed = (jnp.transpose(m * scale) * gain_ref[...]).astype(BF16)
    rows, width = normed.shape
    normed_ref[:, :width] = normed
    if normed_ref.shape[1] > width:
        normed_ref[:, width:] = jnp.zeros((rows, normed_ref.shape[1] - width), BF16)


def mix_and_norm(hidden_t, terms_t, norm_gain):
    width, rows = hidden_t.shape
    normed = jax.ShapeDtypeStruct((rows, -(-width // 128) * 128), BF16)
    return pl.pallas_call(
        mix_kernel,
        out_shape=[jax.ShapeDtypeStruct((width, rows), BF16), normed],
        compiler_params=params(VMEM_MIB),
        name="mix_norm",
    )(hidden_t, *terms_t, norm_gain.reshape(1, width))


def finish_kernel(mixed_ref, *refs):
    parts, out_ref = refs[:-1], refs[-1]
    total = parts[0][...].astype(F32)
    for part in parts[1:]:
        total = total + part[...].astype(F32)
    total = jnp.transpose(total)[: mixed_ref.shape[0]]
    out_ref[...] = (mixed_ref[...].astype(F32) + total).astype(BF16)


def finish(mixed_t, parts):
    return pl.pallas_call(
        finish_kernel,
        out_shape=jax.ShapeDtypeStruct(mixed_t.shape, BF16),
        compiler_params=params(VMEM_MIB),
        name="finish",
    )(mixed_t, *parts)


def pick_kernel(base_s, info_ref, *refs, local):
    count, fields, each = info_ref.shape
    pieces, (x_ref, w_ref, hot_ref) = refs[:count], refs[count:]
    top = fields // 2
    slots = count * CAP
    upper = (
        lax.broadcasted_iota(jnp.int32, (each, each), 0)
        <= lax.broadcasted_iota(jnp.int32, (each, each), 1)
    ).astype(F32).astype(BF16)
    place = lax.broadcasted_iota(jnp.int32, (slots, 1), 0)
    columns, weight = [], 0.0
    for s in range(count):
        route, share = info_ref[s, :top], info_ref[s, top:]
        members, rates = [], []
        for e in range(local):
            hit = route == (base_s[0] + e).astype(F32)
            members.append(jnp.max(jnp.where(hit, 1.0, 0.0), axis=0, keepdims=True))
            rates.append(jnp.sum(jnp.where(hit, share, 0.0), axis=0, keepdims=True))
        member = jnp.concatenate(members, axis=0)
        counts = jnp.dot(member.astype(BF16), upper, preferred_element_type=F32)
        rank = jnp.where(member > 0.0, counts - 1.0, -1000.0).astype(jnp.int32)
        want = place - s * CAP
        hots = [want == rank[e : e + 1] for e in range(local)]
        weight = weight + jnp.concatenate(
            [
                jnp.sum(jnp.where(hots[e], rates[e], 0.0), axis=1, keepdims=True)
                for e in range(local)
            ],
            axis=0,
        )
        columns.append(jnp.concatenate([jnp.where(h, 1.0, 0.0) for h in hots], axis=0))
    for i, s in enumerate(BACK):
        hot_ref[i * each : (i + 1) * each, :] = jnp.transpose(columns[s]).astype(BF16)
    hot = jnp.concatenate([c.astype(BF16) for c in columns], axis=1)
    rows = jnp.concatenate([ref[...] for ref in pieces], axis=0)
    picked = jnp.dot(hot, rows, preferred_element_type=F32).astype(BF16)[:, : x_ref.shape[2]]
    x_ref[...] = picked.reshape(x_ref.shape)
    w_ref[...] = weight.reshape(w_ref.shape)


def pick_rows(base, info, pieces, local, width):
    count, _, each = info.shape
    slots = count * CAP
    smem = pl.BlockSpec(memory_space=pltpu.SMEM)
    vmem = pl.BlockSpec(memory_space=pltpu.VMEM)
    return pl.pallas_call(
        functools.partial(pick_kernel, local=local),
        in_specs=[smem] + [vmem] * (1 + count),
        out_shape=[
            jax.ShapeDtypeStruct((local, slots, width), BF16),
            jax.ShapeDtypeStruct((local, slots, 1), F32),
            jax.ShapeDtypeStruct((count * each, local * slots), BF16),
        ],
        compiler_params=params(VMEM_MIB),
        cost_estimate=pl.CostEstimate(
            flops=4 * local * slots * count * each * width,
            bytes_accessed=2 * (count * each + local * slots) * width,
            transcendentals=0,
        ),
        name="pick",
    )(base, info, *pieces)


def expert_kernel(*refs, groups):
    xs, ws = refs[:groups], refs[groups : 2 * groups]
    up_ref, down_ref = refs[2 * groups : 2 * groups + 2]
    ys, acc_ref = refs[-1 - groups : -1], refs[-1]
    part_at = pl.program_id(1)
    x = jnp.concatenate([ref[0] for ref in xs], axis=0)
    gate = jnp.dot(x, up_ref[0, 0], preferred_element_type=F32)
    up = jnp.dot(x, up_ref[0, 1], preferred_element_type=F32)
    act = ((up + 1.0) * gate * jax.nn.sigmoid(1.702 * gate)).astype(BF16)
    part = lax.dot_general(
        act, down_ref[0], (((1,), (1,)), ((), ())), preferred_element_type=F32
    )

    @pl.when(part_at == 0)
    def _():
        acc_ref[...] = part

    @pl.when(part_at == pl.num_programs(1) - 1)
    def _():
        slots = xs[0].shape[1]
        for i, (w_ref, y_ref) in enumerate(zip(ws, ys)):
            at = slice(i * slots, (i + 1) * slots)
            y_ref[0] = ((acc_ref[at] + part[at]) * w_ref[0]).astype(BF16)


def run_experts(xs, ws, gate_up, down_t, before=(), later=()):
    groups = len(xs)
    local, slots, width = xs[0].shape
    units = gate_up.shape[3]
    splits = 2
    unit = units // splits
    x_spec = pl.BlockSpec((1, slots, width), lambda e, i: (e, 0, 0))
    w_spec = pl.BlockSpec((1, slots, 1), lambda e, i: (e, 0, 0))
    return pl.pallas_call(
        functools.partial(expert_kernel, groups=groups),
        grid=(local, splits),
        in_specs=[
            *[x_spec] * groups,
            *[w_spec] * groups,
            pl.BlockSpec((1, 2, width, unit), lambda e, i: (e, 0, 0, i)),
            pl.BlockSpec((1, width, unit), lambda e, i: (e, 0, i)),
            *[pl.BlockSpec(memory_space=pl.ANY)] * (len(before) + len(later)),
        ],
        out_specs=[pl.BlockSpec(memory_space=pl.ANY)] * len(later) + [x_spec] * groups,
        out_shape=[jax.ShapeDtypeStruct(p.shape, p.dtype) for p in later]
        + [jax.ShapeDtypeStruct((local, slots, width), BF16)] * groups,
        input_output_aliases={2 * groups + 2 + len(before) + i: i for i in range(len(later))},
        scratch_shapes=[pltpu.VMEM((groups * slots, width), F32)],
        compiler_params=params(VMEM_MIB),
        cost_estimate=pl.CostEstimate(
            flops=2 * 2 * 3 * groups * local * slots * width * units,
            bytes_accessed=2 * (gate_up.size + down_t.size + 2 * groups * xs[0].size),
            transcendentals=0,
        ),
        name="experts",
    )(*xs, *ws, gate_up, down_t, *before, *later)


def spread_kernel(hot_ref, y_ref, *refs, adds, skipped):
    y = y_ref[...]
    y = y.reshape(y.shape[0] * y.shape[1], y.shape[2])
    total = jnp.dot(hot_ref[...], y, preferred_element_type=F32)
    width = total.shape[1]
    if adds:
        total = total + refs[0][...][:, :width].astype(F32)
    at = 0
    for ref in refs[adds + skipped :]:
        rows = ref.shape[0]
        ref[:, :width] = total[at : at + rows].astype(BF16)
        if ref.shape[1] > width:
            ref[:, width:] = jnp.zeros((rows, ref.shape[1] - width), BF16)
        at += rows


def spread_rows(hot, y, wide, back=None, before=()):
    rows = hot.shape[0]
    heights = [rows] if back is None else [rows // 2] * 2
    vmem = pl.BlockSpec(memory_space=pltpu.VMEM)
    operands = [hot, y] + ([] if back is None else [back])
    body = functools.partial(
        spread_kernel, adds=0 if back is None else 1, skipped=len(before)
    )
    return pl.pallas_call(
        body,
        in_specs=[vmem] * len(operands) + [pl.BlockSpec(memory_space=pl.ANY)] * len(before),
        out_specs=[vmem] * len(heights),
        out_shape=[jax.ShapeDtypeStruct((h, wide), BF16) for h in heights],
        compiler_params=params(VMEM_MIB),
        cost_estimate=pl.CostEstimate(
            flops=4 * hot.size * wide,
            bytes_accessed=2 * (y.size + 2 * rows * wide),
            transcendentals=0,
        ),
        name="spread",
    )(*operands, *before)


def exchange(value, axes, count, step):
    return lax.ppermute(value, axes, [(i, i ^ step) for i in range(count)])


def add(*terms):
    total = terms[0].astype(F32)
    for term in terms[1:]:
        total = total + term.astype(F32)
    return total.astype(BF16)


def attention_and_norm(
    hidden_in, queries, kv_pages, page_table, new_rows, context, sink_logits, out_proj, norm_gain,
    dp, dp_count, early=None,
):
    me = lax.axis_index(dp)

    def attend(step, before=()):
        col = (me ^ step).astype(jnp.int32).reshape(1)
        part = attend_group(
            col, queries, kv_pages, page_table, new_rows, context, sink_logits, dp_count, before
        )
        return exchange(part, dp, dp_count, step) if step else part

    def project(part):
        term = jnp.dot(part, out_proj, preferred_element_type=F32).astype(BF16)
        return jnp.swapaxes(term, 0, 1)

    order = list(range(dp_count - 1, 0, -1)) + [0]
    parts, terms, back = [], [], []
    for at, step in enumerate(order):
        before = list(terms[-1:]) if at > 1 else []
        if early is not None and step == 0:
            before.append(early)
        parts.append(attend(step, before))
        if at:
            terms.append(project(parts[at - 1]))
            back.append(exchange(terms[-1], dp, dp_count, order[at - 1]))
    terms = back + [project(parts[-1])]
    return mix_and_norm(jnp.swapaxes(hidden_in, 0, 1), terms, norm_gain)


def layer_gathered(
    hidden_in, queries, kv_pages, page_table, new_rows, context, sink_logits, out_proj, norm_gain,
    routes, route_weights, gate_up, down_proj, *, sizes,
):
    ny, nx, nz, nc = sizes
    local, _, width, _ = gate_up.shape
    base = ((lax.axis_index("z") * nc + lax.axis_index("core")) * local).astype(jnp.int32)
    base = base.reshape(1)
    everyone = ("y", "x", "z", "core")
    per_y, per_x = nx * nz * nc, nz * nc
    hops = {"first": (per_x, per_y), "second": (per_y, per_x)}

    def to(value, axis, step=1):
        if axis in hops:
            pairs = [(i, i ^ hops[axis][i % nc]) for i in range(ny * nx * nz * nc)]
            return lax.ppermute(value, everyone, pairs)
        return exchange(value, axis, nz if axis == "z" else nc, step)

    info = jnp.concatenate([routes.astype(F32), route_weights], axis=1)
    info = jnp.swapaxes(info, 0, 1)[None]
    for axis, step in (("first", 1), ("second", 1), ("core", 1), ("z", 1), ("z", 2)):
        info = jnp.concatenate([info, to(info, axis, step)], axis=0)
    info = info.reshape((nz, nc, ny * nx) + info.shape[1:])

    mixed, normed = attention_and_norm(
        hidden_in, queries, kv_pages, page_table, new_rows, context, sink_logits, out_proj,
        norm_gain, ("y", "x"), ny * nx, info,
    )
    wide = normed.shape[1]
    each = normed.shape[0]
    down_t = jnp.swapaxes(down_proj, 1, 2)
    rows = {0: normed, 1: to(normed, "z", 1), 2: to(normed, "z", 2)}
    rows[3] = to(rows[2], "z", 1)
    pairs = ((0, 2), (3, 1))
    near = {r: (to(rows[r], "first"), to(rows[r], "second")) for r in range(nz)}
    hold = pairs[1][0]
    sums, leaves, cames = [], [], []
    for pair in pairs:
        picked = []
        for r in pair:
            plane = [rows[r], *near[r], to(near[r][0], "second")]
            other = [to(piece, "core") for piece in plane]
            for i, pieces in enumerate((plane, other)):
                picked.append(pick_rows(base, info[r, i], pieces, local, width))
        xs, ws, hots = zip(*picked)
        if pair == pairs[0]:
            one, *ys = run_experts(xs, ws, gate_up, down_t, later=[near[hold][0]])
            near[hold] = (one, near[hold][1])
        else:
            ys = run_experts(xs, ws, gate_up, down_t, before=leaves)
        for at, r in enumerate(pair):
            hot, y = hots[2 * at : 2 * at + 2], ys[2 * at : 2 * at + 2]
            first_of_last = pair == pairs[1] and at == 0
            before = list(cames) if first_of_last else ()
            (away,) = spread_rows(hot[1], y[1], wide, before=before)
            leave, keep = spread_rows(hot[0], y[0], wide, to(away, "core"))
            came = to(leave, "second")
            leaves.append(leave)
            cames.append(came)
            last = to(add(keep[each:], came[each:]), "first")
            total = add(keep[:each], came[:each], last)
            sums.append(to(total, "z", r) if r else total)
    return jnp.swapaxes(finish(mixed, sums), 0, 1)


def layer_sent(
    hidden_in, queries, kv_pages, page_table, new_rows, context, sink_logits, out_proj, norm_gain,
    routes, route_weights, gate_up, down_proj, *, dp_count,
):
    row_count, model_width = hidden_in.shape
    mixed, normed = attention_and_norm(
        hidden_in, queries, kv_pages, page_table, new_rows, context, sink_logits, out_proj,
        norm_gain, "dp", dp_count,
    )
    mixed = jnp.swapaxes(mixed, 0, 1)
    normed = normed[:, :model_width]
    assign = routes.reshape(-1)
    onehot = (assign[:, None] == jnp.arange(E, dtype=jnp.int32)[None, :]).astype(jnp.int32)
    slot_index = jnp.sum((jnp.cumsum(onehot, axis=0) - onehot) * onehot, axis=1)
    source = jnp.arange(assign.shape[0], dtype=jnp.int32) // routes.shape[1]
    send_rows = jnp.zeros((E, CAP, model_width), BF16).at[assign, slot_index].set(normed[source])
    copies = jnp.broadcast_to(send_rows[None], (dp_count,) + send_rows.shape)
    copies = copies.reshape(dp_count * E, CAP, model_width)
    everyone = ("dp", "expert")
    blocks = lax.all_to_all(copies, everyone, split_axis=0, concat_axis=0, tiled=True)
    local = gate_up.shape[0]
    shape = blocks.shape
    blocks = blocks.reshape(shape[0] // local, local, CAP, model_width)
    gate_up_f = jnp.einsum("sjcd,jtdf->sjctf", blocks, gate_up, preferred_element_type=F32)
    gate, up = gate_up_f[:, :, :, 0, :], gate_up_f[:, :, :, 1, :]
    hidden = ((up + 1.0) * gate * jax.nn.sigmoid(1.702 * gate)).astype(BF16)
    partials = jnp.einsum("sjcf,jfd->sjcd", hidden, down_proj, preferred_element_type=F32)
    partials = partials.astype(BF16).reshape(shape)
    back = lax.all_to_all(partials, everyone, split_axis=0, concat_axis=0, tiled=True)
    back = jnp.sum(back.reshape(dp_count, E, CAP, model_width).astype(F32), axis=0)
    picked = back[assign, slot_index] * route_weights.reshape(-1)[:, None]
    mix = jnp.sum(picked.reshape(row_count, routes.shape[1], model_width), axis=1)
    return (mixed.astype(F32) + mix).astype(BF16)


def solution(mesh):
    dp_count, expert_count = mesh.shape["dp"], mesh.shape["expert"]
    if dp_count == 4 and expert_count == 8:
        sizes = (2, 2, 4, 2)
        grid = Mesh(mesh.devices.reshape(sizes), ("y", "x", "z", "core"))
        dp, expert, body = ("y", "x"), ("z", "core"), functools.partial(layer_gathered, sizes=sizes)
    else:
        grid = mesh
        dp, expert, body = ("dp",), ("expert",), functools.partial(layer_sent, dp_count=dp_count)
    everyone = dp + expert
    return jax.shard_map(
        body,
        mesh=grid,
        in_specs=(
            P(everyone, None),
            P(everyone, None),
            P(everyone, None, None),
            P(everyone, None),
            P(everyone),
            P(everyone),
            P(),
            P(dp, None),
            P(),
            P(everyone, None),
            P(everyone, None),
            P(expert, None, None, dp),
            P(expert, dp, None),
        ),
        out_specs=P(everyone, None),
        check_vma=False,
    )
```

```python
import functools

import jax
import jax.numpy as jnp
from jax import lax
from jax.experimental import pallas as pl
from jax.experimental.pallas import tpu as pltpu
from jax.sharding import Mesh
from jax.sharding import PartitionSpec as P

QH = 64
KVH = 8
HD = 64
E = 32
CAP = 20
TOP = 4
TERMS = 3
BACK = (2, 3, 0, 1)
GROUP = QH // KVH
TILE = 32
VMEM_MIB = 58

norm_eps = 1e-05
F32 = jnp.float32
BF16 = jnp.bfloat16


def params(mib, **kw):
    return pltpu.CompilerParams(vmem_limit_bytes=mib << 20, **kw)


def attend_kernel(
    col_s, rows_s, ctx_s, table_s, sink_s, q_ref, kv_ref, *refs, kv_heads, reqs, per_req
):
    o_ref = refs[-1]
    page_len = kv_ref.shape[1]
    span = per_req * page_len
    width = 2 * HD
    lane = lax.broadcasted_iota(jnp.int32, (1, width), 1)
    low = lane < HD
    slot = lax.broadcasted_iota(jnp.int32, (1, span), 1)
    row_in = lax.broadcasted_iota(jnp.int32, (TILE, 1), 0)
    head0 = col_s[0] * kv_heads * GROUP

    def one_tile(req, first, last, tile):
        r0 = pl.multiple_of(tile * TILE, TILE)
        row = row_in + r0
        mine = (row >= first) & (row < last)
        limit = jnp.where(mine, row + (ctx_s[req] - last), -1)
        limit = jnp.concatenate([limit] * GROUP, axis=0)
        seen = slot <= limit
        for k in range(kv_heads):
            kv = jnp.concatenate(
                [
                    kv_ref[table_s[req * per_req + p], :, k * width : (k + 1) * width]
                    for p in range(per_req)
                ],
                axis=0,
            )
            parts, sinks = [], []
            for g in range(0, GROUP, 2):
                c0 = (k * GROUP + g) * HD
                pair = q_ref[pl.ds(r0, TILE), c0 : c0 + width].astype(F32) * (HD**-0.5)
                parts.append(jnp.where(low, pair, 0.0).astype(BF16))
                parts.append(jnp.where(low, pltpu.roll(pair, HD, 1), 0.0).astype(BF16))
                for h in (g, g + 1):
                    sinks.append(jnp.full((TILE, 1), sink_s[head0 + k * GROUP + h], F32))
            q = jnp.concatenate(parts, axis=0)
            sink = jnp.concatenate(sinks, axis=0)
            score = lax.dot_general(q, kv, (((1,), (1,)), ((), ())), preferred_element_type=F32)
            score = jnp.where(seen, score, -jnp.inf)
            top = jnp.maximum(jnp.max(score, axis=1, keepdims=True), sink)
            prob = jnp.exp(score - top).astype(BF16)
            ones_v = jnp.where(low, jnp.ones_like(kv), kv)
            both = jnp.dot(prob, ones_v, preferred_element_type=F32)
            swapped = pltpu.roll(both, HD, 1)
            norm = jnp.where(low, both, swapped) + jnp.exp(sink - top)
            out = jnp.where(low, swapped, both) / norm
            for g in range(0, GROUP, 2):
                a = out[g * TILE : (g + 1) * TILE]
                b = out[(g + 1) * TILE : (g + 2) * TILE]
                c0 = (k * GROUP + g) * HD
                old = o_ref[pl.ds(r0, TILE), c0 : c0 + width]
                new = jnp.where(low, a, b).astype(BF16)
                o_ref[pl.ds(r0, TILE), c0 : c0 + width] = jnp.where(mine, new, old)

    def one_req(req, first):
        last = first + rows_s[req]

        def step(tile, carry):
            one_tile(req, first, last, tile)
            return carry

        lax.fori_loop(first // TILE, (last - 1) // TILE + 1, step, 0)
        return last

    lax.fori_loop(0, reqs, one_req, jnp.int32(0))


def attend_group(
    col, queries, kv_pages, page_table, new_rows, context, sink_logits, groups, before=()
):
    rows = queries.shape[0]
    pages, page_len, kv_width = kv_pages.shape
    reqs, per_req = page_table.shape
    kv_heads = KVH // groups
    q_width = queries.shape[1] // groups
    body = functools.partial(attend_kernel, kv_heads=kv_heads, reqs=reqs, per_req=per_req)
    flops = 2 * 2 * rows * q_width * per_req * page_len
    return pl.pallas_call(
        body,
        grid_spec=pltpu.PrefetchScalarGridSpec(
            num_scalar_prefetch=5,
            grid=(1,),
            in_specs=[
                pl.BlockSpec((rows, q_width), lambda i, col, *_: (0, col[0])),
                pl.BlockSpec(
                    (pages, page_len, kv_width // groups), lambda i, col, *_: (0, 0, col[0])
                ),
                *[pl.BlockSpec(memory_space=pl.ANY)] * len(before),
            ],
            out_specs=pl.BlockSpec((rows, q_width), lambda i, *_: (0, 0)),
        ),
        out_shape=jax.ShapeDtypeStruct((rows, q_width), BF16),
        compiler_params=params(VMEM_MIB),
        cost_estimate=pl.CostEstimate(
            flops=8 * flops,
            bytes_accessed=2 * (2 * rows * q_width + pages * page_len * kv_width // groups),
            transcendentals=0,
        ),
        name="attend",
    )(col, new_rows, context, page_table.reshape(-1), sink_logits, queries, kv_pages, *before)


def mix_kernel(x_ref, a_ref, b_ref, c_ref, d_ref, gain_ref, info_ref, mixed_ref, normed_ref):
    total = a_ref[...].astype(F32) + b_ref[...].astype(F32)
    total = total + c_ref[...].astype(F32) + d_ref[...].astype(F32)
    mixed = (x_ref[...].astype(F32) + total).astype(BF16)
    mixed_ref[...] = mixed
    m = mixed.astype(F32)
    scale = lax.rsqrt(jnp.mean(m * m, axis=0, keepdims=True) + norm_eps)
    normed = (jnp.transpose(m * scale) * gain_ref[...]).astype(BF16)
    rows, width = normed.shape
    normed_ref[:, :width] = normed
    fill = normed_ref.shape[1] - width
    if fill:
        lane = lax.broadcasted_iota(jnp.int32, (rows, 128), 1) - (128 - fill)
        rest = info_ref[...]
        info = rest.astype(BF16).astype(F32)
        for i in range(1, TERMS):
            rest = rest - rest.astype(BF16).astype(F32)
            moved = pltpu.roll(rest.astype(BF16).astype(F32), i * TOP, 1)
            info = jnp.where((lane >= (i + 1) * TOP) & (lane < (i + 2) * TOP), moved, info)
        normed_ref[:, width:] = info[:, 128 - fill :].astype(BF16)


def mix_and_norm(hidden_t, terms_t, norm_gain, routes, route_weights):
    width, rows = hidden_t.shape
    fill = -width % 128
    info = jnp.concatenate([routes.astype(F32), route_weights], axis=1)
    info = jnp.pad(info, ((0, 0), (128 - fill, fill - info.shape[1]))) if fill else jnp.zeros((rows, 128))
    normed = jax.ShapeDtypeStruct((rows, -(-width // 128) * 128), BF16)
    return pl.pallas_call(
        mix_kernel,
        out_shape=[jax.ShapeDtypeStruct((width, rows), BF16), normed],
        compiler_params=params(VMEM_MIB),
        name="mix_norm",
    )(hidden_t, *terms_t, norm_gain.reshape(1, width), info)


def finish_kernel(mixed_ref, *refs):
    parts, out_ref = refs[:-1], refs[-1]
    total = parts[0][...].astype(F32)
    for part in parts[1:]:
        total = total + part[...].astype(F32)
    total = jnp.transpose(total)[: mixed_ref.shape[0]]
    out_ref[...] = (mixed_ref[...].astype(F32) + total).astype(BF16)


def finish(mixed_t, parts):
    return pl.pallas_call(
        finish_kernel,
        out_shape=jax.ShapeDtypeStruct(mixed_t.shape, BF16),
        compiler_params=params(VMEM_MIB),
        name="finish",
    )(mixed_t, *parts)


def pick_kernel(bases_s, *refs, count, local, width):
    pieces, (x_ref, far_ref, hot_ref) = refs[:count], refs[-3:]
    each, wide = pieces[0].shape
    slots = count * CAP
    both = 2 * local
    at = width - (wide - 128)
    upper = (
        lax.broadcasted_iota(jnp.int32, (each, each), 0)
        <= lax.broadcasted_iota(jnp.int32, (each, each), 1)
    ).astype(F32).astype(BF16)
    members = []
    for s in range(count):
        info = jnp.transpose(pieces[s][:, wide - 128 :].astype(F32))[at : at + TOP]
        for e in range(both):
            expert = (bases_s[e // local] + e % local).astype(F32)
            members.append(jnp.max(jnp.where(info == expert, 1.0, 0.0), axis=0, keepdims=True))
    member = jnp.concatenate(members, axis=0)
    counts = jnp.dot(member.astype(BF16), upper, preferred_element_type=F32)
    rank = jnp.where(member > 0.0, counts - 1.0, -100.0)
    place = lax.broadcasted_iota(jnp.int32, (slots, each), 0).astype(F32)
    columns = []
    for s in range(count):
        want = place - float(s * CAP)
        hots = [
            jnp.where(want == rank[s * both + e : s * both + e + 1], 1.0, 0.0) for e in range(both)
        ]
        columns.append(jnp.concatenate(hots, axis=0).astype(BF16))
    hot = jnp.concatenate(columns, axis=1)
    rows = jnp.concatenate([ref[...] for ref in pieces], axis=0)
    half = local * slots
    for i, ref in enumerate((x_ref, far_ref)):
        picked = jnp.dot(hot[i * half : (i + 1) * half], rows, preferred_element_type=F32)
        ref[...] = picked.astype(BF16).reshape(ref.shape)
    rank_t = jnp.transpose(rank).astype(BF16)
    slot = lax.broadcasted_iota(jnp.int32, (count * both, both * slots), 1)
    line = lax.broadcasted_iota(jnp.int32, (count * both, both * slots), 0)
    for i, s in enumerate(BACK):
        first = (line - s * both) * slots
        owner = (slot >= first) & (slot < first + slots) & (line >= s * both)
        owner = owner & (line < (s + 1) * both)
        owner = jnp.where(owner, 1.0, 0.0)
        want = slot[:1] - s * CAP - jnp.sum(
            jnp.where(owner > 0.0, line - s * both, 0), axis=0, keepdims=True
        ) * slots
        held = jnp.dot(rank_t, owner.astype(BF16), preferred_element_type=F32)
        hot_ref[i * each : (i + 1) * each, :] = jnp.where(held == want.astype(F32), 1.0, 0.0).astype(
            BF16
        )


def pick_rows(bases, pieces, local, width, before=(), later=()):
    count = len(pieces)
    each, wide = pieces[0].shape
    slots = count * CAP
    smem = pl.BlockSpec(memory_space=pltpu.SMEM)
    vmem = pl.BlockSpec(memory_space=pltpu.VMEM)
    hand_on = pl.BlockSpec(memory_space=pl.ANY)
    x = jax.ShapeDtypeStruct((local, slots, wide), BF16)
    return pl.pallas_call(
        functools.partial(pick_kernel, count=count, local=local, width=width),
        in_specs=[smem] + [vmem] * count + [hand_on] * (len(before) + len(later)),
        out_specs=[hand_on] * len(later) + [vmem] * 3,
        out_shape=[jax.ShapeDtypeStruct(p.shape, p.dtype) for p in later]
        + [x, x, jax.ShapeDtypeStruct((count * each, 2 * local * slots), BF16)],
        input_output_aliases={1 + count + len(before) + i: i for i in range(len(later))},
        compiler_params=params(VMEM_MIB),
        cost_estimate=pl.CostEstimate(
            flops=2 * 4 * local * slots * count * each * wide,
            bytes_accessed=2 * (count * each + 2 * local * slots) * wide,
            transcendentals=0,
        ),
        name="pick",
    )(bases, *pieces, *before, *later)


def expert_kernel(bases_s, *refs, groups):
    xs, (up_ref, down_ref) = refs[:groups], refs[groups : groups + 2]
    ys, acc_ref = refs[-1 - groups : -1], refs[-1]
    part_at = pl.program_id(1)
    width = down_ref.shape[1]
    wide = xs[0].shape[2]
    x = jnp.concatenate([ref[0] for ref in xs], axis=0)
    gate = jnp.dot(x[:, :width], up_ref[0, 0], preferred_element_type=F32)
    up = jnp.dot(x[:, :width], up_ref[0, 1], preferred_element_type=F32)
    act = ((up + 1.0) * gate * jax.nn.sigmoid(1.702 * gate)).astype(BF16)
    part = lax.dot_general(
        act, down_ref[0], (((1,), (1,)), ((), ())), preferred_element_type=F32
    )

    @pl.when(part_at == 0)
    def _():
        acc_ref[...] = part

    @pl.when(part_at == pl.num_programs(1) - 1)
    def _():
        info = x[:, wide - 128 :].astype(F32)
        lane = lax.broadcasted_iota(jnp.int32, info.shape, 1) - (width - (wide - 128))
        share = 0.0
        for i in range(TERMS):
            share = share + pltpu.roll(info, 128 - (i + 1) * TOP, 1)
        expert = (bases_s[0] + pl.program_id(0)).astype(F32)
        mine = (lane >= 0) & (lane < TOP) & (info == expert)
        share = jnp.sum(jnp.where(mine, share, 0.0), axis=1, keepdims=True)
        slots = xs[0].shape[1]
        for i, y_ref in enumerate(ys):
            at = slice(i * slots, (i + 1) * slots)
            y_ref[0, :, :width] = ((acc_ref[at] + part[at]) * share[at]).astype(BF16)
            if wide > width:
                y_ref[0, :, width:] = jnp.zeros((slots, wide - width), BF16)


def run_experts(bases, xs, gate_up, down_t, before=(), later=()):
    groups = len(xs)
    local, slots, wide = xs[0].shape
    width, units = gate_up.shape[2:]
    splits = 2
    unit = units // splits
    x_spec = pl.BlockSpec((1, slots, wide), lambda e, i: (e, 0, 0))
    hand_on = pl.BlockSpec(memory_space=pl.ANY)
    return pl.pallas_call(
        functools.partial(expert_kernel, groups=groups),
        grid=(local, splits),
        in_specs=[
            pl.BlockSpec(memory_space=pltpu.SMEM),
            *[x_spec] * groups,
            pl.BlockSpec((1, 2, width, unit), lambda e, i: (e, 0, 0, i)),
            pl.BlockSpec((1, width, unit), lambda e, i: (e, 0, i)),
            *[hand_on] * (len(before) + len(later)),
        ],
        out_specs=[hand_on] * len(later) + [x_spec] * groups,
        out_shape=[jax.ShapeDtypeStruct(p.shape, p.dtype) for p in later]
        + [jax.ShapeDtypeStruct((local, slots, wide), BF16)] * groups,
        input_output_aliases={3 + groups + len(before) + i: i for i in range(len(later))},
        scratch_shapes=[pltpu.VMEM((groups * slots, width), F32)],
        compiler_params=params(VMEM_MIB),
        cost_estimate=pl.CostEstimate(
            flops=2 * 2 * 3 * groups * local * slots * width * units,
            bytes_accessed=2 * (gate_up.size + down_t.size + 2 * groups * xs[0].size),
            transcendentals=0,
        ),
        name="experts",
    )(bases, *xs, gate_up, down_t, *before, *later)


def spread_kernel(hot_ref, mine_ref, far_ref, *refs):
    leave_ref, keep_ref = refs[-2:]
    local, slots, wide = mine_ref.shape
    y = [ref[...].reshape(local * slots, wide) for ref in (mine_ref, far_ref)]
    y = jnp.concatenate(y, axis=0)
    half = leave_ref.shape[0]
    for i, ref in enumerate((leave_ref, keep_ref)):
        hot = hot_ref[i * half : (i + 1) * half, :]
        ref[...] = jnp.dot(hot, y, preferred_element_type=F32).astype(BF16)


def spread_rows(hot, mine, far, before=()):
    rows = hot.shape[0]
    wide = mine.shape[2]
    vmem = pl.BlockSpec(memory_space=pltpu.VMEM)
    return pl.pallas_call(
        spread_kernel,
        in_specs=[vmem] * 3 + [pl.BlockSpec(memory_space=pl.ANY)] * len(before),
        out_specs=[vmem] * 2,
        out_shape=[jax.ShapeDtypeStruct((rows // 2, wide), BF16)] * 2,
        compiler_params=params(VMEM_MIB),
        cost_estimate=pl.CostEstimate(
            flops=4 * hot.size * wide,
            bytes_accessed=2 * (2 * mine.size + rows * wide),
            transcendentals=0,
        ),
        name="spread",
    )(hot, mine, far, *before)


def exchange(value, axes, count, step):
    return lax.ppermute(value, axes, [(i, i ^ step) for i in range(count)])


def add(*terms):
    total = terms[0].astype(F32)
    for term in terms[1:]:
        total = total + term.astype(F32)
    return total.astype(BF16)


def attention_and_norm(
    hidden_in, queries, kv_pages, page_table, new_rows, context, sink_logits, out_proj, norm_gain,
    routes, route_weights, dp, dp_count,
):
    me = lax.axis_index(dp)

    def attend(step, before=()):
        col = (me ^ step).astype(jnp.int32).reshape(1)
        part = attend_group(
            col, queries, kv_pages, page_table, new_rows, context, sink_logits, dp_count, before
        )
        return exchange(part, dp, dp_count, step) if step else part

    def project(part):
        term = jnp.dot(part, out_proj, preferred_element_type=F32).astype(BF16)
        return jnp.swapaxes(term, 0, 1)

    order = list(range(dp_count - 1, 0, -1)) + [0]
    parts, terms, back = [], [], []
    for at, step in enumerate(order):
        before = list(terms[-1:]) if at > 1 else []
        parts.append(attend(step, before))
        if at:
            terms.append(project(parts[at - 1]))
            back.append(exchange(terms[-1], dp, dp_count, order[at - 1]))
    terms = back + [project(parts[-1])]
    hidden_t = jnp.swapaxes(hidden_in, 0, 1)
    return mix_and_norm(hidden_t, terms, norm_gain, routes, route_weights)


def layer_gathered(
    hidden_in, queries, kv_pages, page_table, new_rows, context, sink_logits, out_proj, norm_gain,
    routes, route_weights, gate_up, down_proj, *, sizes,
):
    ny, nx, nz, nc = sizes
    local, _, width, _ = gate_up.shape
    core = lax.axis_index("core")
    bases = (lax.axis_index("z") * nc + jnp.stack([core, core ^ 1])) * local
    bases = bases.astype(jnp.int32)
    everyone = ("y", "x", "z", "core")
    per_y, per_x = nx * nz * nc, nz * nc
    hops = {"first": (per_x, per_y), "second": (per_y, per_x)}

    def to(value, axis, step=1):
        if axis in hops:
            pairs = [(i, i ^ hops[axis][i % nc]) for i in range(ny * nx * nz * nc)]
            return lax.ppermute(value, everyone, pairs)
        return exchange(value, axis, nz if axis == "z" else nc, step)

    mixed, normed = attention_and_norm(
        hidden_in, queries, kv_pages, page_table, new_rows, context, sink_logits, out_proj,
        norm_gain, routes, route_weights, ("y", "x"), ny * nx,
    )
    each = normed.shape[0]
    down_t = jnp.swapaxes(down_proj, 1, 2)
    rows = {0: normed, 1: to(normed, "z", 1), 2: to(normed, "z", 2)}
    pairs = ((0, 2), (3, 1))
    near, sums, cames = {}, [], []
    for pair in pairs:
        xs, hots = [], []
        for r in pair:
            if r not in near:
                near[r] = (to(rows[r], "first"), to(rows[r], "second"))
            plane = [rows[r], *near[r], to(near[r][0], "second")]
            if r == 0:
                later = [rows[1], rows[2]]
                rows[1], rows[2], x, far, hot = pick_rows(bases, plane, local, width, (), later)
                rows[3] = to(rows[2], "z", 1)
                near[1] = (to(rows[1], "first"), to(rows[1], "second"))
            elif r == 2:
                rows[3], x, far, hot = pick_rows(bases, plane, local, width, (), [rows[3]])
                near[3] = (to(rows[3], "first"), to(rows[3], "second"))
            else:
                x, far, hot = pick_rows(bases, plane, local, width)
            xs += [x, to(far, "core")]
            hots.append(hot)
        if pair == pairs[0]:
            ys = run_experts(bases, xs, gate_up, down_t)
        else:
            ys = run_experts(bases, xs, gate_up, down_t, before=cames)
        for at, r in enumerate(pair):
            y, far = ys[2 * at], to(ys[2 * at + 1], "core")
            leave, keep = spread_rows(hots[at], y, far)
            came = to(leave, "second")
            cames.append(came)
            last = to(add(keep[each:], came[each:]), "first")
            total = add(keep[:each], came[:each], last)
            sums.append(to(total, "z", r) if r else total)
    return jnp.swapaxes(finish(mixed, sums), 0, 1)


def layer_sent(
    hidden_in, queries, kv_pages, page_table, new_rows, context, sink_logits, out_proj, norm_gain,
    routes, route_weights, gate_up, down_proj, *, dp_count,
):
    row_count, model_width = hidden_in.shape
    mixed, normed = attention_and_norm(
        hidden_in, queries, kv_pages, page_table, new_rows, context, sink_logits, out_proj,
        norm_gain, routes, route_weights, "dp", dp_count,
    )
    mixed = jnp.swapaxes(mixed, 0, 1)
    normed = normed[:, :model_width]
    assign = routes.reshape(-1)
    onehot = (assign[:, None] == jnp.arange(E, dtype=jnp.int32)[None, :]).astype(jnp.int32)
    slot_index = jnp.sum((jnp.cumsum(onehot, axis=0) - onehot) * onehot, axis=1)
    source = jnp.arange(assign.shape[0], dtype=jnp.int32) // routes.shape[1]
    send_rows = jnp.zeros((E, CAP, model_width), BF16).at[assign, slot_index].set(normed[source])
    copies = jnp.broadcast_to(send_rows[None], (dp_count,) + send_rows.shape)
    copies = copies.reshape(dp_count * E, CAP, model_width)
    everyone = ("dp", "expert")
    blocks = lax.all_to_all(copies, everyone, split_axis=0, concat_axis=0, tiled=True)
    local = gate_up.shape[0]
    shape = blocks.shape
    blocks = blocks.reshape(shape[0] // local, local, CAP, model_width)
    gate_up_f = jnp.einsum("sjcd,jtdf->sjctf", blocks, gate_up, preferred_element_type=F32)
    gate, up = gate_up_f[:, :, :, 0, :], gate_up_f[:, :, :, 1, :]
    hidden = ((up + 1.0) * gate * jax.nn.sigmoid(1.702 * gate)).astype(BF16)
    partials = jnp.einsum("sjcf,jfd->sjcd", hidden, down_proj, preferred_element_type=F32)
    partials = partials.astype(BF16).reshape(shape)
    back = lax.all_to_all(partials, everyone, split_axis=0, concat_axis=0, tiled=True)
    back = jnp.sum(back.reshape(dp_count, E, CAP, model_width).astype(F32), axis=0)
    picked = back[assign, slot_index] * route_weights.reshape(-1)[:, None]
    mix = jnp.sum(picked.reshape(row_count, routes.shape[1], model_width), axis=1)
    return (mixed.astype(F32) + mix).astype(BF16)


def solution(mesh):
    dp_count, expert_count = mesh.shape["dp"], mesh.shape["expert"]
    if dp_count == 4 and expert_count == 8:
        sizes = (2, 2, 4, 2)
        grid = Mesh(mesh.devices.reshape(sizes), ("y", "x", "z", "core"))
        dp, expert, body = ("y", "x"), ("z", "core"), functools.partial(layer_gathered, sizes=sizes)
    else:
        grid = mesh
        dp, expert, body = ("dp",), ("expert",), functools.partial(layer_sent, dp_count=dp_count)
    everyone = dp + expert
    return jax.shard_map(
        body,
        mesh=grid,
        in_specs=(
            P(everyone, None),
            P(everyone, None),
            P(everyone, None, None),
            P(everyone, None),
            P(everyone),
            P(everyone),
            P(),
            P(dp, None),
            P(),
            P(everyone, None),
            P(everyone, None),
            P(expert, None, None, dp),
            P(expert, dp, None),
        ),
        out_specs=P(everyone, None),
        check_vma=False,
    )
```

```python
import functools

import jax
import jax.numpy as jnp
from jax import lax
from jax.experimental import pallas as pl
from jax.experimental.pallas import tpu as pltpu
from jax.sharding import Mesh
from jax.sharding import PartitionSpec as P

QH = 64
KVH = 8
HD = 64
E = 32
CAP = 20
TOP = 4
TERMS = 3
BACK = (2, 3, 0, 1)
GROUP = QH // KVH
TILE = 32
VMEM_MIB = 58

norm_eps = 1e-05
F32 = jnp.float32
BF16 = jnp.bfloat16


def params(mib, **kw):
    return pltpu.CompilerParams(vmem_limit_bytes=mib << 20, **kw)


def attend_kernel(
    col_s, rows_s, ctx_s, table_s, sink_s, q_ref, kv_ref, *refs, kv_heads, reqs, per_req
):
    o_ref = refs[-1]
    page_len = kv_ref.shape[1]
    span = per_req * page_len
    width = 2 * HD
    lane = lax.broadcasted_iota(jnp.int32, (1, width), 1)
    low = lane < HD
    slot = lax.broadcasted_iota(jnp.int32, (1, span), 1)
    row_in = lax.broadcasted_iota(jnp.int32, (TILE, 1), 0)
    head0 = col_s[0] * kv_heads * GROUP

    def one_tile(req, first, last, tile):
        r0 = pl.multiple_of(tile * TILE, TILE)
        row = row_in + r0
        mine = (row >= first) & (row < last)
        limit = jnp.where(mine, row + (ctx_s[req] - last), -1)
        limit = jnp.concatenate([limit] * GROUP, axis=0)
        seen = slot <= limit
        for k in range(kv_heads):
            kv = jnp.concatenate(
                [
                    kv_ref[table_s[req * per_req + p], :, k * width : (k + 1) * width]
                    for p in range(per_req)
                ],
                axis=0,
            )
            parts, sinks = [], []
            for g in range(0, GROUP, 2):
                c0 = (k * GROUP + g) * HD
                pair = q_ref[pl.ds(r0, TILE), c0 : c0 + width].astype(F32) * (HD**-0.5)
                parts.append(jnp.where(low, pair, 0.0).astype(BF16))
                parts.append(jnp.where(low, pltpu.roll(pair, HD, 1), 0.0).astype(BF16))
                for h in (g, g + 1):
                    sinks.append(jnp.full((TILE, 1), sink_s[head0 + k * GROUP + h], F32))
            q = jnp.concatenate(parts, axis=0)
            sink = jnp.concatenate(sinks, axis=0)
            score = lax.dot_general(q, kv, (((1,), (1,)), ((), ())), preferred_element_type=F32)
            score = jnp.where(seen, score, -jnp.inf)
            top = jnp.maximum(jnp.max(score, axis=1, keepdims=True), sink)
            prob = jnp.exp(score - top).astype(BF16)
            ones_v = jnp.where(low, jnp.ones_like(kv), kv)
            both = jnp.dot(prob, ones_v, preferred_element_type=F32)
            swapped = pltpu.roll(both, HD, 1)
            norm = jnp.where(low, both, swapped) + jnp.exp(sink - top)
            out = jnp.where(low, swapped, both) / norm
            for g in range(0, GROUP, 2):
                a = out[g * TILE : (g + 1) * TILE]
                b = out[(g + 1) * TILE : (g + 2) * TILE]
                c0 = (k * GROUP + g) * HD
                old = o_ref[pl.ds(r0, TILE), c0 : c0 + width]
                new = jnp.where(low, a, b).astype(BF16)
                o_ref[pl.ds(r0, TILE), c0 : c0 + width] = jnp.where(mine, new, old)

    def one_req(req, first):
        last = first + rows_s[req]

        def step(tile, carry):
            one_tile(req, first, last, tile)
            return carry

        lax.fori_loop(first // TILE, (last - 1) // TILE + 1, step, 0)
        return last

    lax.fori_loop(0, reqs, one_req, jnp.int32(0))


def attend_group(
    col, queries, kv_pages, page_table, new_rows, context, sink_logits, groups, before=()
):
    rows = queries.shape[0]
    pages, page_len, kv_width = kv_pages.shape
    reqs, per_req = page_table.shape
    kv_heads = KVH // groups
    q_width = queries.shape[1] // groups
    body = functools.partial(attend_kernel, kv_heads=kv_heads, reqs=reqs, per_req=per_req)
    flops = 2 * 2 * rows * q_width * per_req * page_len
    return pl.pallas_call(
        body,
        grid_spec=pltpu.PrefetchScalarGridSpec(
            num_scalar_prefetch=5,
            grid=(1,),
            in_specs=[
                pl.BlockSpec((rows, q_width), lambda i, col, *_: (0, col[0])),
                pl.BlockSpec(
                    (pages, page_len, kv_width // groups), lambda i, col, *_: (0, 0, col[0])
                ),
                *[pl.BlockSpec(memory_space=pl.ANY)] * len(before),
            ],
            out_specs=pl.BlockSpec((rows, q_width), lambda i, *_: (0, 0)),
        ),
        out_shape=jax.ShapeDtypeStruct((rows, q_width), BF16),
        compiler_params=params(VMEM_MIB),
        cost_estimate=pl.CostEstimate(
            flops=8 * flops,
            bytes_accessed=2 * (2 * rows * q_width + pages * page_len * kv_width // groups),
            transcendentals=0,
        ),
        name="attend",
    )(col, new_rows, context, page_table.reshape(-1), sink_logits, queries, kv_pages, *before)


def mix_kernel(x_ref, a_ref, b_ref, c_ref, d_ref, gain_ref, info_ref, mixed_ref, normed_ref):
    total = a_ref[...].astype(F32) + b_ref[...].astype(F32)
    total = total + c_ref[...].astype(F32) + d_ref[...].astype(F32)
    mixed = (x_ref[...].astype(F32) + total).astype(BF16)
    mixed_ref[...] = mixed
    m = mixed.astype(F32)
    scale = lax.rsqrt(jnp.mean(m * m, axis=0, keepdims=True) + norm_eps)
    normed = (jnp.transpose(m * scale) * gain_ref[...]).astype(BF16)
    rows, width = normed.shape
    normed_ref[:, :width] = normed
    fill = normed_ref.shape[1] - width
    if fill:
        lane = lax.broadcasted_iota(jnp.int32, (rows, 128), 1) - (128 - fill)
        rest = info_ref[...]
        info = rest.astype(BF16).astype(F32)
        for i in range(1, TERMS):
            rest = rest - rest.astype(BF16).astype(F32)
            moved = pltpu.roll(rest.astype(BF16).astype(F32), i * TOP, 1)
            info = jnp.where((lane >= (i + 1) * TOP) & (lane < (i + 2) * TOP), moved, info)
        normed_ref[:, width:] = info[:, 128 - fill :].astype(BF16)


def mix_and_norm(hidden_t, terms_t, norm_gain, routes, route_weights):
    width, rows = hidden_t.shape
    fill = -width % 128
    info = jnp.concatenate([routes.astype(F32), route_weights], axis=1)
    info = jnp.pad(info, ((0, 0), (128 - fill, fill - info.shape[1]))) if fill else jnp.zeros((rows, 128))
    normed = jax.ShapeDtypeStruct((rows, -(-width // 128) * 128), BF16)
    return pl.pallas_call(
        mix_kernel,
        out_shape=[jax.ShapeDtypeStruct((width, rows), BF16), normed],
        compiler_params=params(VMEM_MIB),
        name="mix_norm",
    )(hidden_t, *terms_t, norm_gain.reshape(1, width), info)


def finish_kernel(mixed_ref, *refs):
    parts, out_ref = refs[:-1], refs[-1]
    total = parts[0][...].astype(F32)
    for part in parts[1:]:
        total = total + part[...].astype(F32)
    total = jnp.transpose(total)[: mixed_ref.shape[0]]
    out_ref[...] = (mixed_ref[...].astype(F32) + total).astype(BF16)


def finish(mixed_t, parts):
    return pl.pallas_call(
        finish_kernel,
        out_shape=jax.ShapeDtypeStruct(mixed_t.shape, BF16),
        compiler_params=params(VMEM_MIB),
        name="finish",
    )(mixed_t, *parts)


def pick_kernel(bases_s, *refs, count, local, width):
    pieces, (x_ref, far_ref, hot_ref) = refs[:count], refs[-3:]
    each, wide = pieces[0].shape
    slots = count * CAP
    both = 2 * local
    at = width - (wide - 128)
    upper = (
        lax.broadcasted_iota(jnp.int32, (each, each), 0)
        <= lax.broadcasted_iota(jnp.int32, (each, each), 1)
    ).astype(F32).astype(BF16)
    members = []
    for s in range(count):
        info = jnp.transpose(pieces[s][:, wide - 128 :].astype(F32))[at : at + TOP]
        for e in range(both):
            expert = (bases_s[e // local] + e % local).astype(F32)
            members.append(jnp.max(jnp.where(info == expert, 1.0, 0.0), axis=0, keepdims=True))
    member = jnp.concatenate(members, axis=0)
    counts = jnp.dot(member.astype(BF16), upper, preferred_element_type=F32)
    rank = jnp.where(member > 0.0, counts - 1.0, -100.0)
    place = lax.broadcasted_iota(jnp.int32, (slots, each), 0).astype(F32)
    columns = []
    for s in range(count):
        want = place - float(s * CAP)
        hots = [
            jnp.where(want == rank[s * both + e : s * both + e + 1], 1.0, 0.0) for e in range(both)
        ]
        columns.append(jnp.concatenate(hots, axis=0).astype(BF16))
    hot = jnp.concatenate(columns, axis=1)
    rows = jnp.concatenate([ref[...] for ref in pieces], axis=0)
    half = local * slots
    for i, ref in enumerate((x_ref, far_ref)):
        picked = jnp.dot(hot[i * half : (i + 1) * half], rows, preferred_element_type=F32)
        ref[...] = picked.astype(BF16).reshape(ref.shape)
    rank_t = jnp.transpose(rank).astype(BF16)
    slot = lax.broadcasted_iota(jnp.int32, (count * both, both * slots), 1)
    line = lax.broadcasted_iota(jnp.int32, (count * both, both * slots), 0)
    for i, s in enumerate(BACK):
        first = (line - s * both) * slots
        owner = (slot >= first) & (slot < first + slots) & (line >= s * both)
        owner = owner & (line < (s + 1) * both)
        owner = jnp.where(owner, 1.0, 0.0)
        want = slot[:1] - s * CAP - jnp.sum(
            jnp.where(owner > 0.0, line - s * both, 0), axis=0, keepdims=True
        ) * slots
        held = jnp.dot(rank_t, owner.astype(BF16), preferred_element_type=F32)
        hot_ref[i * each : (i + 1) * each, :] = jnp.where(held == want.astype(F32), 1.0, 0.0).astype(
            BF16
        )


def pick_rows(bases, pieces, local, width, before=(), later=()):
    count = len(pieces)
    each, wide = pieces[0][0].shape
    slots = count * CAP
    smem = pl.BlockSpec(memory_space=pltpu.SMEM)
    vmem = pl.BlockSpec(memory_space=pltpu.VMEM)
    hand_on = pl.BlockSpec(memory_space=pl.ANY)
    spots = [pl.BlockSpec((each, wide), functools.partial(lambda at, i: (at, 0), at)) for _, at in pieces]
    x = jax.ShapeDtypeStruct((local, slots, wide), BF16)
    return pl.pallas_call(
        functools.partial(pick_kernel, count=count, local=local, width=width),
        grid=(1,),
        in_specs=[smem] + spots + [hand_on] * (len(before) + len(later)),
        out_specs=[hand_on] * len(later) + [vmem] * 3,
        out_shape=[jax.ShapeDtypeStruct(p.shape, p.dtype) for p in later]
        + [x, x, jax.ShapeDtypeStruct((count * each, 2 * local * slots), BF16)],
        input_output_aliases={1 + count + len(before) + i: i for i in range(len(later))},
        compiler_params=params(VMEM_MIB),
        cost_estimate=pl.CostEstimate(
            flops=2 * 4 * local * slots * count * each * wide,
            bytes_accessed=2 * (count * each + 2 * local * slots) * wide,
            transcendentals=0,
        ),
        name="pick",
    )(bases, *[piece for piece, _ in pieces], *before, *later)


def expert_kernel(bases_s, *refs, groups, far_parts):
    xs, (up_ref, down_ref) = refs[:groups], refs[groups : groups + 2]
    mine_ref, far_refs, acc_ref = refs[-2 - far_parts], refs[-1 - far_parts : -1], refs[-1]
    part_at = pl.program_id(1)
    width = down_ref.shape[1]
    wide = xs[0].shape[2]
    x = jnp.concatenate([ref[0] for ref in xs], axis=0)
    gate = jnp.dot(x[:, :width], up_ref[0, 0], preferred_element_type=F32)
    up = jnp.dot(x[:, :width], up_ref[0, 1], preferred_element_type=F32)
    act = ((up + 1.0) * gate * jax.nn.sigmoid(1.702 * gate)).astype(BF16)
    part = lax.dot_general(
        act, down_ref[0], (((1,), (1,)), ((), ())), preferred_element_type=F32
    )

    @pl.when(part_at == 0)
    def _():
        acc_ref[...] = part

    @pl.when(part_at == pl.num_programs(1) - 1)
    def _():
        info = x[:, wide - 128 :].astype(F32)
        lane = lax.broadcasted_iota(jnp.int32, info.shape, 1) - (width - (wide - 128))
        share = 0.0
        for i in range(TERMS):
            share = share + pltpu.roll(info, 128 - (i + 1) * TOP, 1)
        expert = (bases_s[0] + pl.program_id(0)).astype(F32)
        mine = (lane >= 0) & (lane < TOP) & (info == expert)
        share = jnp.sum(jnp.where(mine, share, 0.0), axis=1, keepdims=True)
        slots = xs[0].shape[1]
        per_far = groups // 2 // far_parts
        for i in range(groups):
            at = slice(i * slots, (i + 1) * slots)
            y = ((acc_ref[at] + part[at]) * share[at]).astype(BF16)
            chunk = i // 2
            y_ref, place = (far_refs[chunk // per_far], chunk % per_far) if i % 2 else (mine_ref, chunk)
            to = slice(place * slots, (place + 1) * slots)
            y_ref[0, to, :width] = y
            if wide > width:
                y_ref[0, to, width:] = jnp.zeros((slots, wide - width), BF16)


def run_experts(bases, xs, gate_up, down_t, far_parts):
    groups = len(xs)
    local, slots, wide = xs[0].shape
    width, units = gate_up.shape[2:]
    splits = 2
    unit = units // splits
    heights = [groups // 2 * slots] + [groups // 2 // far_parts * slots] * far_parts
    return pl.pallas_call(
        functools.partial(expert_kernel, groups=groups, far_parts=far_parts),
        grid=(local, splits),
        in_specs=[
            pl.BlockSpec(memory_space=pltpu.SMEM),
            *[pl.BlockSpec((1, slots, wide), lambda e, i: (e, 0, 0))] * groups,
            pl.BlockSpec((1, 2, width, unit), lambda e, i: (e, 0, 0, i)),
            pl.BlockSpec((1, width, unit), lambda e, i: (e, 0, i)),
        ],
        out_specs=[pl.BlockSpec((1, h, wide), lambda e, i: (e, 0, 0)) for h in heights],
        out_shape=[jax.ShapeDtypeStruct((local, h, wide), BF16) for h in heights],
        scratch_shapes=[pltpu.VMEM((groups * slots, width), F32)],
        compiler_params=params(VMEM_MIB),
        cost_estimate=pl.CostEstimate(
            flops=2 * 2 * 3 * groups * local * slots * width * units,
            bytes_accessed=2 * (gate_up.size + down_t.size + 2 * groups * xs[0].size),
            transcendentals=0,
        ),
        name="experts",
    )(bases, *xs, gate_up, down_t)


def spread_kernel(*refs, count):
    hots, (mine_ref, far_ref) = refs[:count], refs[count : count + 2]
    leave_ref, keep_ref = refs[-2:]
    each = hots[0].shape[0] // len(BACK)
    local, slots, wide = mine_ref.shape
    slots = slots // count
    for c in range(count):
        y = [
            ref[:, c * slots : (c + 1) * slots, :].reshape(local * slots, wide)
            for ref in (mine_ref, far_ref)
        ]
        y = jnp.concatenate(y, axis=0)
        for i in range(2):
            hot = hots[c][2 * i * each : 2 * (i + 1) * each, :]
            total = jnp.dot(hot, y, preferred_element_type=F32).astype(BF16)
            for j in range(2):
                at = (j * count + c) * each
                ref = (leave_ref, keep_ref)[i]
                ref[at : at + each, :] = total[j * each : (j + 1) * each]


def spread_rows(hots, mine, far, first, before=()):
    count = len(hots)
    rows, depth = hots[0].shape
    local, height, wide = far.shape
    vmem = pl.BlockSpec(memory_space=pltpu.VMEM)
    return pl.pallas_call(
        functools.partial(spread_kernel, count=count),
        grid=(1,),
        in_specs=[vmem] * count
        + [pl.BlockSpec((local, height, wide), lambda i: (0, first // count, 0)), vmem]
        + [pl.BlockSpec(memory_space=pl.ANY)] * len(before),
        out_specs=[vmem] * 2,
        out_shape=[jax.ShapeDtypeStruct((count * rows // 2, wide), BF16)] * 2,
        compiler_params=params(VMEM_MIB),
        cost_estimate=pl.CostEstimate(
            flops=4 * count * rows * depth * wide,
            bytes_accessed=2 * (2 * far.size + count * rows * wide),
            transcendentals=0,
        ),
        name="spread",
    )(*hots, mine, far, *before)


def exchange(value, axes, count, step):
    return lax.ppermute(value, axes, [(i, i ^ step) for i in range(count)])


def add(*terms):
    total = terms[0].astype(F32)
    for term in terms[1:]:
        total = total + term.astype(F32)
    return total.astype(BF16)


def turn_kernel(keep_ref, came_ref, *refs):
    refs[-1][...] = add(keep_ref[...], came_ref[...])


def turn_rows(keep, came, before):
    rows, wide = keep.shape
    half = pl.BlockSpec((rows // 2, wide), lambda i: (1, 0))
    return pl.pallas_call(
        turn_kernel,
        grid=(1,),
        in_specs=[half, half] + [pl.BlockSpec(memory_space=pl.ANY)] * len(before),
        out_specs=pl.BlockSpec((rows // 2, wide), lambda i: (0, 0)),
        out_shape=jax.ShapeDtypeStruct((rows // 2, wide), BF16),
        compiler_params=params(VMEM_MIB),
        name="turn",
    )(keep, came, *before)


def attention_and_norm(
    hidden_in, queries, kv_pages, page_table, new_rows, context, sink_logits, out_proj, norm_gain,
    routes, route_weights, dp, dp_count,
):
    me = lax.axis_index(dp)

    def attend(step, before=()):
        col = (me ^ step).astype(jnp.int32).reshape(1)
        part = attend_group(
            col, queries, kv_pages, page_table, new_rows, context, sink_logits, dp_count, before
        )
        return exchange(part, dp, dp_count, step) if step else part

    def project(part):
        term = jnp.dot(part, out_proj, preferred_element_type=F32).astype(BF16)
        return jnp.swapaxes(term, 0, 1)

    order = list(range(dp_count - 1, 0, -1)) + [0]
    parts, terms, back = [], [], []
    for at, step in enumerate(order):
        before = list(terms[-1:]) if at > 1 else []
        parts.append(attend(step, before))
        if at:
            terms.append(project(parts[at - 1]))
            back.append(exchange(terms[-1], dp, dp_count, order[at - 1]))
    terms = back + [project(parts[-1])]
    hidden_t = jnp.swapaxes(hidden_in, 0, 1)
    return mix_and_norm(hidden_t, terms, norm_gain, routes, route_weights)


def layer_gathered(
    hidden_in, queries, kv_pages, page_table, new_rows, context, sink_logits, out_proj, norm_gain,
    routes, route_weights, gate_up, down_proj, *, sizes,
):
    ny, nx, nz, nc = sizes
    local, _, width, _ = gate_up.shape
    core = lax.axis_index("core")
    bases = (lax.axis_index("z") * nc + jnp.stack([core, core ^ 1])) * local
    bases = bases.astype(jnp.int32)
    everyone = ("y", "x", "z", "core")
    per_y, per_x = nx * nz * nc, nz * nc
    hops = {"first": (per_x, per_y), "second": (per_y, per_x)}

    def to(value, axis, step=1):
        if axis in hops:
            pairs = [(i, i ^ hops[axis][i % nc]) for i in range(ny * nx * nz * nc)]
            return lax.ppermute(value, everyone, pairs)
        return exchange(value, axis, nz if axis == "z" else nc, step)

    mixed, normed = attention_and_norm(
        hidden_in, queries, kv_pages, page_table, new_rows, context, sink_logits, out_proj,
        norm_gain, routes, route_weights, ("y", "x"), ny * nx,
    )
    each = normed.shape[0]
    down_t = jnp.swapaxes(down_proj, 1, 2)
    rows = {0: normed, 1: to(normed, "z", 1), 2: to(normed, "z", 2)}

    def gather(values):
        one = to(values, "first")
        return values, one, to(values, "second"), to(one, "second")

    def pick(r, arrays, at, **order):
        pieces = [(rows[r], 0)] + [(array, at) for array in arrays[1:]]
        *later, x, far, hot = pick_rows(bases, pieces, local, width, **order)
        return later, [x, to(far, "core")], hot

    def reduce(hots, mine, far, first, before=(), turn_before=()):
        count = len(hots)
        half = count * each
        leave, keep = spread_rows(hots, mine, to(far, "core"), first, before)
        came = to(leave, "second")
        if turn_before:
            last = to(turn_rows(keep, came, turn_before), "first")
        else:
            last = to(add(keep[half:], came[half:]), "first")
        parts = [slice(c * each, (c + 1) * each) for c in range(count)]
        return [add(keep[at], came[at], last[at]) for at in parts], last

    (rows[1], rows[2]), x_0, hot_0 = pick(0, gather(rows[0]), 0, later=[rows[1], rows[2]])
    rows[3] = to(rows[2], "z", 1)
    (rows[3],), x_2, hot_2 = pick(2, gather(rows[2]), 0, later=[rows[3]])
    mine, far = run_experts(bases, x_0 + x_2, gate_up, down_t, 1)
    (sum_0, sum_2), last = reduce([hot_0, hot_2], mine, far, 0)
    plane = gather(jnp.concatenate([rows[3], rows[1]], axis=0))
    _, x_3, hot_3 = pick(3, plane, 0)
    _, x_1, hot_1 = pick(1, plane, 1)
    mine, far_3, far_1 = run_experts(bases, x_3 + x_1, gate_up, down_t, 2)
    sum_2 = to(sum_2, "z", 2)
    (sum_3,), _ = reduce([hot_3], mine, far_3, 0)
    (sum_1,), _ = reduce([hot_1], mine, far_1, 1, [last], [sum_2])
    sums = [sum_0, sum_2, to(sum_3, "z", 3), to(sum_1, "z", 1)]
    return jnp.swapaxes(finish(mixed, sums), 0, 1)


def layer_sent(
    hidden_in, queries, kv_pages, page_table, new_rows, context, sink_logits, out_proj, norm_gain,
    routes, route_weights, gate_up, down_proj, *, dp_count,
):
    row_count, model_width = hidden_in.shape
    mixed, normed = attention_and_norm(
        hidden_in, queries, kv_pages, page_table, new_rows, context, sink_logits, out_proj,
        norm_gain, routes, route_weights, "dp", dp_count,
    )
    mixed = jnp.swapaxes(mixed, 0, 1)
    normed = normed[:, :model_width]
    assign = routes.reshape(-1)
    onehot = (assign[:, None] == jnp.arange(E, dtype=jnp.int32)[None, :]).astype(jnp.int32)
    slot_index = jnp.sum((jnp.cumsum(onehot, axis=0) - onehot) * onehot, axis=1)
    source = jnp.arange(assign.shape[0], dtype=jnp.int32) // routes.shape[1]
    send_rows = jnp.zeros((E, CAP, model_width), BF16).at[assign, slot_index].set(normed[source])
    copies = jnp.broadcast_to(send_rows[None], (dp_count,) + send_rows.shape)
    copies = copies.reshape(dp_count * E, CAP, model_width)
    everyone = ("dp", "expert")
    blocks = lax.all_to_all(copies, everyone, split_axis=0, concat_axis=0, tiled=True)
    local = gate_up.shape[0]
    shape = blocks.shape
    blocks = blocks.reshape(shape[0] // local, local, CAP, model_width)
    gate_up_f = jnp.einsum("sjcd,jtdf->sjctf", blocks, gate_up, preferred_element_type=F32)
    gate, up = gate_up_f[:, :, :, 0, :], gate_up_f[:, :, :, 1, :]
    hidden = ((up + 1.0) * gate * jax.nn.sigmoid(1.702 * gate)).astype(BF16)
    partials = jnp.einsum("sjcf,jfd->sjcd", hidden, down_proj, preferred_element_type=F32)
    partials = partials.astype(BF16).reshape(shape)
    back = lax.all_to_all(partials, everyone, split_axis=0, concat_axis=0, tiled=True)
    back = jnp.sum(back.reshape(dp_count, E, CAP, model_width).astype(F32), axis=0)
    picked = back[assign, slot_index] * route_weights.reshape(-1)[:, None]
    mix = jnp.sum(picked.reshape(row_count, routes.shape[1], model_width), axis=1)
    return (mixed.astype(F32) + mix).astype(BF16)


def solution(mesh):
    dp_count, expert_count = mesh.shape["dp"], mesh.shape["expert"]
    if dp_count == 4 and expert_count == 8:
        sizes = (2, 2, 4, 2)
        grid = Mesh(mesh.devices.reshape(sizes), ("y", "x", "z", "core"))
        dp, expert, body = ("y", "x"), ("z", "core"), functools.partial(layer_gathered, sizes=sizes)
    else:
        grid = mesh
        dp, expert, body = ("dp",), ("expert",), functools.partial(layer_sent, dp_count=dp_count)
    everyone = dp + expert
    return jax.shard_map(
        body,
        mesh=grid,
        in_specs=(
            P(everyone, None),
            P(everyone, None),
            P(everyone, None, None),
            P(everyone, None),
            P(everyone),
            P(everyone),
            P(),
            P(dp, None),
            P(),
            P(everyone, None),
            P(everyone, None),
            P(expert, None, None, dp),
            P(expert, dp, None),
        ),
        out_specs=P(everyone, None),
        check_vma=False,
    )
```

```python
import functools

import jax
import jax.numpy as jnp
from jax import lax
from jax.experimental import pallas as pl
from jax.experimental.pallas import tpu as pltpu
from jax.sharding import Mesh
from jax.sharding import PartitionSpec as P

QH = 64
KVH = 8
HD = 64
E = 32
CAP = 20
TOP = 4
TERMS = 3
BACK = (2, 3, 0, 1)
GROUP = QH // KVH
TILE = 32
VMEM_MIB = 58

norm_eps = 1e-05
F32 = jnp.float32
BF16 = jnp.bfloat16


def params(mib, **kw):
    return pltpu.CompilerParams(vmem_limit_bytes=mib << 20, **kw)


def attend_kernel(
    col_s, rows_s, ctx_s, table_s, sink_s, q_ref, kv_ref, *refs, kv_heads, reqs, per_req
):
    o_ref = refs[-1]
    page_len = kv_ref.shape[1]
    span = per_req * page_len
    width = 2 * HD
    lane = lax.broadcasted_iota(jnp.int32, (1, width), 1)
    low = lane < HD
    slot = lax.broadcasted_iota(jnp.int32, (1, span), 1)
    row_in = lax.broadcasted_iota(jnp.int32, (TILE, 1), 0)
    head0 = col_s[0] * kv_heads * GROUP

    def one_tile(req, first, last, tile):
        r0 = pl.multiple_of(tile * TILE, TILE)
        row = row_in + r0
        mine = (row >= first) & (row < last)
        limit = jnp.where(mine, row + (ctx_s[req] - last), -1)
        limit = jnp.concatenate([limit] * GROUP, axis=0)
        seen = slot <= limit
        for k in range(kv_heads):
            kv = jnp.concatenate(
                [
                    kv_ref[table_s[req * per_req + p], :, k * width : (k + 1) * width]
                    for p in range(per_req)
                ],
                axis=0,
            )
            parts, sinks = [], []
            for g in range(0, GROUP, 2):
                c0 = (k * GROUP + g) * HD
                pair = q_ref[pl.ds(r0, TILE), c0 : c0 + width].astype(F32) * (HD**-0.5)
                parts.append(jnp.where(low, pair, 0.0).astype(BF16))
                parts.append(jnp.where(low, pltpu.roll(pair, HD, 1), 0.0).astype(BF16))
                for h in (g, g + 1):
                    sinks.append(jnp.full((TILE, 1), sink_s[head0 + k * GROUP + h], F32))
            q = jnp.concatenate(parts, axis=0)
            sink = jnp.concatenate(sinks, axis=0)
            score = lax.dot_general(q, kv, (((1,), (1,)), ((), ())), preferred_element_type=F32)
            score = jnp.where(seen, score, -jnp.inf)
            top = jnp.maximum(jnp.max(score, axis=1, keepdims=True), sink)
            prob = jnp.exp(score - top).astype(BF16)
            ones_v = jnp.where(low, jnp.ones_like(kv), kv)
            both = jnp.dot(prob, ones_v, preferred_element_type=F32)
            swapped = pltpu.roll(both, HD, 1)
            norm = jnp.where(low, both, swapped) + jnp.exp(sink - top)
            out = jnp.where(low, swapped, both) / norm
            for g in range(0, GROUP, 2):
                a = out[g * TILE : (g + 1) * TILE]
                b = out[(g + 1) * TILE : (g + 2) * TILE]
                c0 = (k * GROUP + g) * HD
                old = o_ref[pl.ds(r0, TILE), c0 : c0 + width]
                new = jnp.where(low, a, b).astype(BF16)
                o_ref[pl.ds(r0, TILE), c0 : c0 + width] = jnp.where(mine, new, old)

    def one_req(req, first):
        last = first + rows_s[req]

        def step(tile, carry):
            one_tile(req, first, last, tile)
            return carry

        lax.fori_loop(first // TILE, (last - 1) // TILE + 1, step, 0)
        return last

    lax.fori_loop(0, reqs, one_req, jnp.int32(0))


def attend_group(
    col, queries, kv_pages, page_table, new_rows, context, sink_logits, groups, before=()
):
    rows = queries.shape[0]
    pages, page_len, kv_width = kv_pages.shape
    reqs, per_req = page_table.shape
    kv_heads = KVH // groups
    q_width = queries.shape[1] // groups
    body = functools.partial(attend_kernel, kv_heads=kv_heads, reqs=reqs, per_req=per_req)
    flops = 2 * 2 * rows * q_width * per_req * page_len
    return pl.pallas_call(
        body,
        grid_spec=pltpu.PrefetchScalarGridSpec(
            num_scalar_prefetch=5,
            grid=(1,),
            in_specs=[
                pl.BlockSpec((rows, q_width), lambda i, col, *_: (0, col[0])),
                pl.BlockSpec(
                    (pages, page_len, kv_width // groups), lambda i, col, *_: (0, 0, col[0])
                ),
                *[pl.BlockSpec(memory_space=pl.ANY)] * len(before),
            ],
            out_specs=pl.BlockSpec((rows, q_width), lambda i, *_: (0, 0)),
        ),
        out_shape=jax.ShapeDtypeStruct((rows, q_width), BF16),
        compiler_params=params(VMEM_MIB),
        cost_estimate=pl.CostEstimate(
            flops=8 * flops,
            bytes_accessed=2 * (2 * rows * q_width + pages * page_len * kv_width // groups),
            transcendentals=0,
        ),
        name="attend",
    )(col, new_rows, context, page_table.reshape(-1), sink_logits, queries, kv_pages, *before)


def mix_kernel(x_ref, a_ref, b_ref, c_ref, d_ref, gain_ref, info_ref, mixed_ref, normed_ref):
    total = a_ref[...].astype(F32) + b_ref[...].astype(F32)
    total = total + c_ref[...].astype(F32) + d_ref[...].astype(F32)
    mixed = (x_ref[...].astype(F32) + total).astype(BF16)
    mixed_ref[...] = mixed
    m = mixed.astype(F32)
    scale = lax.rsqrt(jnp.mean(m * m, axis=0, keepdims=True) + norm_eps)
    normed = (jnp.transpose(m * scale) * gain_ref[...]).astype(BF16)
    rows, width = normed.shape
    normed_ref[:, :width] = normed
    fill = normed_ref.shape[1] - width
    if fill:
        lane = lax.broadcasted_iota(jnp.int32, (rows, 128), 1) - (128 - fill)
        rest = info_ref[...]
        info = rest.astype(BF16).astype(F32)
        for i in range(1, TERMS):
            rest = rest - rest.astype(BF16).astype(F32)
            moved = pltpu.roll(rest.astype(BF16).astype(F32), i * TOP, 1)
            info = jnp.where((lane >= (i + 1) * TOP) & (lane < (i + 2) * TOP), moved, info)
        normed_ref[:, width:] = info[:, 128 - fill :].astype(BF16)


def mix_and_norm(hidden_t, terms_t, norm_gain, routes, route_weights):
    width, rows = hidden_t.shape
    fill = -width % 128
    info = jnp.concatenate([routes.astype(F32), route_weights], axis=1)
    info = jnp.pad(info, ((0, 0), (128 - fill, fill - info.shape[1]))) if fill else jnp.zeros((rows, 128))
    normed = jax.ShapeDtypeStruct((rows, -(-width // 128) * 128), BF16)
    return pl.pallas_call(
        mix_kernel,
        out_shape=[jax.ShapeDtypeStruct((width, rows), BF16), normed],
        compiler_params=params(VMEM_MIB),
        name="mix_norm",
    )(hidden_t, *terms_t, norm_gain.reshape(1, width), info)


def finish_kernel(mixed_ref, *refs):
    parts, out_ref = refs[:-1], refs[-1]
    total = parts[0][...].astype(F32)
    for part in parts[1:]:
        total = total + part[...].astype(F32)
    total = jnp.transpose(total)[: mixed_ref.shape[0]]
    out_ref[...] = (mixed_ref[...].astype(F32) + total).astype(BF16)


def finish(mixed_t, parts):
    return pl.pallas_call(
        finish_kernel,
        out_shape=jax.ShapeDtypeStruct(mixed_t.shape, BF16),
        compiler_params=params(VMEM_MIB),
        name="finish",
    )(mixed_t, *parts)


def pick_kernel(bases_s, *refs, count, local, width):
    pieces, (x_ref, far_ref, hot_ref) = refs[:count], refs[-3:]
    each, wide = pieces[0].shape
    slots = count * CAP
    both = 2 * local
    at = width - (wide - 128)
    upper = (
        lax.broadcasted_iota(jnp.int32, (each, each), 0)
        <= lax.broadcasted_iota(jnp.int32, (each, each), 1)
    ).astype(F32).astype(BF16)
    members = []
    for s in range(count):
        info = jnp.transpose(pieces[s][:, wide - 128 :].astype(F32))[at : at + TOP]
        for e in range(both):
            expert = (bases_s[e // local] + e % local).astype(F32)
            members.append(jnp.max(jnp.where(info == expert, 1.0, 0.0), axis=0, keepdims=True))
    member = jnp.concatenate(members, axis=0)
    counts = jnp.dot(member.astype(BF16), upper, preferred_element_type=F32)
    rank = jnp.where(member > 0.0, counts - 1.0, -100.0)
    place = lax.broadcasted_iota(jnp.int32, (slots, each), 0).astype(F32)
    columns = []
    for s in range(count):
        want = place - float(s * CAP)
        hots = [
            jnp.where(want == rank[s * both + e : s * both + e + 1], 1.0, 0.0) for e in range(both)
        ]
        columns.append(jnp.concatenate(hots, axis=0).astype(BF16))
    hot = jnp.concatenate(columns, axis=1)
    rows = jnp.concatenate([ref[...] for ref in pieces], axis=0)
    half = local * slots
    for i, ref in enumerate((x_ref, far_ref)):
        picked = jnp.dot(hot[i * half : (i + 1) * half], rows, preferred_element_type=F32)
        ref[...] = picked.astype(BF16).reshape(ref.shape)
    rank_t = jnp.transpose(rank).astype(BF16)
    slot = lax.broadcasted_iota(jnp.int32, (count * both, both * slots), 1)
    line = lax.broadcasted_iota(jnp.int32, (count * both, both * slots), 0)
    for i, s in enumerate(BACK):
        first = (line - s * both) * slots
        owner = (slot >= first) & (slot < first + slots) & (line >= s * both)
        owner = owner & (line < (s + 1) * both)
        owner = jnp.where(owner, 1.0, 0.0)
        want = slot[:1] - s * CAP - jnp.sum(
            jnp.where(owner > 0.0, line - s * both, 0), axis=0, keepdims=True
        ) * slots
        held = jnp.dot(rank_t, owner.astype(BF16), preferred_element_type=F32)
        hot_ref[i * each : (i + 1) * each, :] = jnp.where(held == want.astype(F32), 1.0, 0.0).astype(
            BF16
        )


def pick_rows(bases, pieces, local, width, before=(), later=()):
    count = len(pieces)
    each, wide = pieces[0][0].shape
    slots = count * CAP
    smem = pl.BlockSpec(memory_space=pltpu.SMEM)
    vmem = pl.BlockSpec(memory_space=pltpu.VMEM)
    hand_on = pl.BlockSpec(memory_space=pl.ANY)
    spots = [pl.BlockSpec((each, wide), functools.partial(lambda at, i: (at, 0), at)) for _, at in pieces]
    x = jax.ShapeDtypeStruct((local, slots, wide), BF16)
    return pl.pallas_call(
        functools.partial(pick_kernel, count=count, local=local, width=width),
        grid=(1,),
        in_specs=[smem] + spots + [hand_on] * (len(before) + len(later)),
        out_specs=[hand_on] * len(later) + [vmem] * 3,
        out_shape=[jax.ShapeDtypeStruct(p.shape, p.dtype) for p in later]
        + [x, x, jax.ShapeDtypeStruct((count * each, 2 * local * slots), BF16)],
        input_output_aliases={1 + count + len(before) + i: i for i in range(len(later))},
        compiler_params=params(VMEM_MIB),
        cost_estimate=pl.CostEstimate(
            flops=2 * 4 * local * slots * count * each * wide,
            bytes_accessed=2 * (count * each + 2 * local * slots) * wide,
            transcendentals=0,
        ),
        name="pick",
    )(bases, *[piece for piece, _ in pieces], *before, *later)


def expert_kernel(bases_s, *refs, groups, far_parts):
    xs, (up_ref, down_ref) = refs[:groups], refs[groups : groups + 2]
    mine_ref, far_refs = refs[-1 - far_parts], refs[len(refs) - far_parts :]
    width = down_ref.shape[1]
    wide = xs[0].shape[2]
    x = jnp.concatenate([ref[0] for ref in xs], axis=0)
    gate = jnp.dot(x[:, :width], up_ref[0, 0], preferred_element_type=F32)
    up = jnp.dot(x[:, :width], up_ref[0, 1], preferred_element_type=F32)
    act = ((up + 1.0) * gate * jax.nn.sigmoid(1.702 * gate)).astype(BF16)
    part = lax.dot_general(
        act, down_ref[0], (((1,), (1,)), ((), ())), preferred_element_type=F32
    )
    info = x[:, wide - 128 :].astype(F32)
    lane = lax.broadcasted_iota(jnp.int32, info.shape, 1) - (width - (wide - 128))
    share = 0.0
    for i in range(TERMS):
        share = share + pltpu.roll(info, 128 - (i + 1) * TOP, 1)
    expert = (bases_s[0] + pl.program_id(0)).astype(F32)
    mine = (lane >= 0) & (lane < TOP) & (info == expert)
    share = jnp.sum(jnp.where(mine, share, 0.0), axis=1, keepdims=True)
    slots = xs[0].shape[1]
    per_far = groups // 2 // far_parts
    for i in range(groups):
        at = slice(i * slots, (i + 1) * slots)
        y = (part[at] * share[at]).astype(BF16)
        chunk = i // 2
        y_ref, place = (far_refs[chunk // per_far], chunk % per_far) if i % 2 else (mine_ref, chunk)
        to = slice(place * slots, (place + 1) * slots)
        y_ref[0, to, :width] = y
        if wide > width:
            y_ref[0, to, width:] = jnp.zeros((slots, wide - width), BF16)


def run_experts(bases, xs, gate_up, down_t, far_parts):
    groups = len(xs)
    local, slots, wide = xs[0].shape
    width, units = gate_up.shape[2:]
    heights = [groups // 2 * slots] + [groups // 2 // far_parts * slots] * far_parts
    return pl.pallas_call(
        functools.partial(expert_kernel, groups=groups, far_parts=far_parts),
        grid=(local,),
        in_specs=[
            pl.BlockSpec(memory_space=pltpu.SMEM),
            *[pl.BlockSpec((1, slots, wide), lambda e: (e, 0, 0))] * groups,
            pl.BlockSpec((1, 2, width, units), lambda e: (e, 0, 0, 0)),
            pl.BlockSpec((1, width, units), lambda e: (e, 0, 0)),
        ],
        out_specs=[pl.BlockSpec((1, h, wide), lambda e: (e, 0, 0)) for h in heights],
        out_shape=[jax.ShapeDtypeStruct((local, h, wide), BF16) for h in heights],
        compiler_params=params(VMEM_MIB),
        cost_estimate=pl.CostEstimate(
            flops=2 * 2 * 3 * groups * local * slots * width * units,
            bytes_accessed=2 * (gate_up.size + down_t.size + 2 * groups * xs[0].size),
            transcendentals=0,
        ),
        name="experts",
    )(bases, *xs, gate_up, down_t)


def spread_kernel(*refs, count):
    hots, (mine_ref, far_ref) = refs[:count], refs[count : count + 2]
    leave_ref, keep_ref = refs[-2:]
    each = hots[0].shape[0] // len(BACK)
    local, slots, wide = mine_ref.shape
    slots = slots // count
    for c in range(count):
        y = [
            ref[:, c * slots : (c + 1) * slots, :].reshape(local * slots, wide)
            for ref in (mine_ref, far_ref)
        ]
        y = jnp.concatenate(y, axis=0)
        for i in range(2):
            hot = hots[c][2 * i * each : 2 * (i + 1) * each, :]
            total = jnp.dot(hot, y, preferred_element_type=F32).astype(BF16)
            for j in range(2):
                at = (j * count + c) * each
                ref = (leave_ref, keep_ref)[i]
                ref[at : at + each, :] = total[j * each : (j + 1) * each]


def spread_rows(hots, mine, far, first):
    count = len(hots)
    rows, depth = hots[0].shape
    local, height, wide = far.shape
    vmem = pl.BlockSpec(memory_space=pltpu.VMEM)
    return pl.pallas_call(
        functools.partial(spread_kernel, count=count),
        grid=(1,),
        in_specs=[vmem] * count
        + [pl.BlockSpec((local, height, wide), lambda i: (0, first // count, 0)), vmem],
        out_specs=[vmem] * 2,
        out_shape=[jax.ShapeDtypeStruct((count * rows // 2, wide), BF16)] * 2,
        compiler_params=params(VMEM_MIB),
        cost_estimate=pl.CostEstimate(
            flops=4 * count * rows * depth * wide,
            bytes_accessed=2 * (2 * far.size + count * rows * wide),
            transcendentals=0,
        ),
        name="spread",
    )(*hots, mine, far)


def exchange(value, axes, count, step):
    return lax.ppermute(value, axes, [(i, i ^ step) for i in range(count)])


def add(*terms):
    total = terms[0].astype(F32)
    for term in terms[1:]:
        total = total + term.astype(F32)
    return total.astype(BF16)


def together_kernel(*refs):
    pass


def together(*arrays):
    return pl.pallas_call(
        together_kernel,
        in_specs=[pl.BlockSpec(memory_space=pl.ANY)] * len(arrays),
        out_specs=[pl.BlockSpec(memory_space=pl.ANY)] * len(arrays),
        out_shape=[jax.ShapeDtypeStruct(a.shape, a.dtype) for a in arrays],
        input_output_aliases={i: i for i in range(len(arrays))},
        name="together",
    )(*arrays)


def turn_kernel(keep_ref, came_ref, *refs):
    refs[-1][...] = add(keep_ref[...], came_ref[...])


def turn_rows(keep, came, before):
    rows, wide = keep.shape
    half = pl.BlockSpec((rows // 2, wide), lambda i: (1, 0))
    return pl.pallas_call(
        turn_kernel,
        grid=(1,),
        in_specs=[half, half] + [pl.BlockSpec(memory_space=pl.ANY)] * len(before),
        out_specs=pl.BlockSpec((rows // 2, wide), lambda i: (0, 0)),
        out_shape=jax.ShapeDtypeStruct((rows // 2, wide), BF16),
        compiler_params=params(VMEM_MIB),
        name="turn",
    )(keep, came, *before)


def attention_and_norm(
    hidden_in, queries, kv_pages, page_table, new_rows, context, sink_logits, out_proj, norm_gain,
    routes, route_weights, dp, dp_count,
):
    me = lax.axis_index(dp)

    def attend(step, before=()):
        col = (me ^ step).astype(jnp.int32).reshape(1)
        part = attend_group(
            col, queries, kv_pages, page_table, new_rows, context, sink_logits, dp_count, before
        )
        return exchange(part, dp, dp_count, step) if step else part

    def project(part):
        term = jnp.dot(part, out_proj, preferred_element_type=F32).astype(BF16)
        return jnp.swapaxes(term, 0, 1)

    order = list(range(dp_count - 1, 0, -1)) + [0]
    parts, terms, back = [], [], []
    for at, step in enumerate(order):
        before = list(terms[-1:]) if at > 1 else []
        parts.append(attend(step, before))
        if at:
            terms.append(project(parts[at - 1]))
            back.append(exchange(terms[-1], dp, dp_count, order[at - 1]))
    terms = back + [project(parts[-1])]
    hidden_t = jnp.swapaxes(hidden_in, 0, 1)
    return mix_and_norm(hidden_t, terms, norm_gain, routes, route_weights)


def layer_gathered(
    hidden_in, queries, kv_pages, page_table, new_rows, context, sink_logits, out_proj, norm_gain,
    routes, route_weights, gate_up, down_proj, *, sizes,
):
    ny, nx, nz, nc = sizes
    local, _, width, _ = gate_up.shape
    core = lax.axis_index("core")
    bases = (lax.axis_index("z") * nc + jnp.stack([core, core ^ 1])) * local
    bases = bases.astype(jnp.int32)
    everyone = ("y", "x", "z", "core")
    per_y, per_x = nx * nz * nc, nz * nc
    hops = {"first": (per_x, per_y), "second": (per_y, per_x)}

    def to(value, axis, step=1):
        if axis in hops:
            pairs = [(i, i ^ hops[axis][i % nc]) for i in range(ny * nx * nz * nc)]
            return lax.ppermute(value, everyone, pairs)
        return exchange(value, axis, nz if axis == "z" else nc, step)

    mixed, normed = attention_and_norm(
        hidden_in, queries, kv_pages, page_table, new_rows, context, sink_logits, out_proj,
        norm_gain, routes, route_weights, ("y", "x"), ny * nx,
    )
    each = normed.shape[0]
    down_t = jnp.swapaxes(down_proj, 1, 2)
    rows = {0: normed, 1: to(normed, "z", 1), 2: to(normed, "z", 2)}

    def gather(values, both=False):
        one, two = to(values, "first"), to(values, "second")
        if both:
            one, two = together(one, two)
        return values, one, two, to(one, "second")

    def pick(r, arrays, at, **order):
        pieces = [(rows[r], 0)] + [(array, at) for array in arrays[1:]]
        *later, x, far, hot = pick_rows(bases, pieces, local, width, **order)
        return later, [x, to(far, "core")], hot

    def reduce(hots, mine, far, first, turn_before=()):
        count = len(hots)
        half = count * each
        leave, keep = spread_rows(hots, mine, to(far, "core"), first)
        came = to(leave, "second")
        if turn_before:
            last = to(turn_rows(keep, came, turn_before), "first")
        else:
            last = to(add(keep[half:], came[half:]), "first")
        parts = [slice(c * each, (c + 1) * each) for c in range(count)]
        return [add(keep[at], came[at], last[at]) for at in parts], last

    (rows[1], rows[2]), x_0, hot_0 = pick(0, gather(rows[0]), 0, later=[rows[1], rows[2]])
    rows[3] = to(rows[2], "z", 1)
    (rows[3],), x_2, hot_2 = pick(2, gather(rows[2]), 0, later=[rows[3]])
    mine, far = run_experts(bases, x_0 + x_2, gate_up, down_t, 1)
    (sum_0, sum_2), last = reduce([hot_0, hot_2], mine, far, 0)
    plane = gather(jnp.concatenate([rows[3], rows[1]], axis=0), both=True)
    _, x_3, hot_3 = pick(3, plane, 0)
    _, x_1, hot_1 = pick(1, plane, 1)
    mine, far_3, far_1 = run_experts(bases, x_3 + x_1, gate_up, down_t, 2)
    sum_2 = to(sum_2, "z", 2)
    (sum_3,), _ = reduce([hot_3], mine, far_3, 0)
    (sum_1,), _ = reduce([hot_1], mine, far_1, 1, [sum_2])
    sums = [sum_0, sum_2, to(sum_3, "z", 3), to(sum_1, "z", 1)]
    return jnp.swapaxes(finish(mixed, sums), 0, 1)


def layer_sent(
    hidden_in, queries, kv_pages, page_table, new_rows, context, sink_logits, out_proj, norm_gain,
    routes, route_weights, gate_up, down_proj, *, dp_count,
):
    row_count, model_width = hidden_in.shape
    mixed, normed = attention_and_norm(
        hidden_in, queries, kv_pages, page_table, new_rows, context, sink_logits, out_proj,
        norm_gain, routes, route_weights, "dp", dp_count,
    )
    mixed = jnp.swapaxes(mixed, 0, 1)
    normed = normed[:, :model_width]
    assign = routes.reshape(-1)
    onehot = (assign[:, None] == jnp.arange(E, dtype=jnp.int32)[None, :]).astype(jnp.int32)
    slot_index = jnp.sum((jnp.cumsum(onehot, axis=0) - onehot) * onehot, axis=1)
    source = jnp.arange(assign.shape[0], dtype=jnp.int32) // routes.shape[1]
    send_rows = jnp.zeros((E, CAP, model_width), BF16).at[assign, slot_index].set(normed[source])
    copies = jnp.broadcast_to(send_rows[None], (dp_count,) + send_rows.shape)
    copies = copies.reshape(dp_count * E, CAP, model_width)
    everyone = ("dp", "expert")
    blocks = lax.all_to_all(copies, everyone, split_axis=0, concat_axis=0, tiled=True)
    local = gate_up.shape[0]
    shape = blocks.shape
    blocks = blocks.reshape(shape[0] // local, local, CAP, model_width)
    gate_up_f = jnp.einsum("sjcd,jtdf->sjctf", blocks, gate_up, preferred_element_type=F32)
    gate, up = gate_up_f[:, :, :, 0, :], gate_up_f[:, :, :, 1, :]
    hidden = ((up + 1.0) * gate * jax.nn.sigmoid(1.702 * gate)).astype(BF16)
    partials = jnp.einsum("sjcf,jfd->sjcd", hidden, down_proj, preferred_element_type=F32)
    partials = partials.astype(BF16).reshape(shape)
    back = lax.all_to_all(partials, everyone, split_axis=0, concat_axis=0, tiled=True)
    back = jnp.sum(back.reshape(dp_count, E, CAP, model_width).astype(F32), axis=0)
    picked = back[assign, slot_index] * route_weights.reshape(-1)[:, None]
    mix = jnp.sum(picked.reshape(row_count, routes.shape[1], model_width), axis=1)
    return (mixed.astype(F32) + mix).astype(BF16)


def solution(mesh):
    dp_count, expert_count = mesh.shape["dp"], mesh.shape["expert"]
    if dp_count == 4 and expert_count == 8:
        sizes = (2, 2, 4, 2)
        grid = Mesh(mesh.devices.reshape(sizes), ("y", "x", "z", "core"))
        dp, expert, body = ("y", "x"), ("z", "core"), functools.partial(layer_gathered, sizes=sizes)
    else:
        grid = mesh
        dp, expert, body = ("dp",), ("expert",), functools.partial(layer_sent, dp_count=dp_count)
    everyone = dp + expert
    return jax.shard_map(
        body,
        mesh=grid,
        in_specs=(
            P(everyone, None),
            P(everyone, None),
            P(everyone, None, None),
            P(everyone, None),
            P(everyone),
            P(everyone),
            P(),
            P(dp, None),
            P(),
            P(everyone, None),
            P(everyone, None),
            P(expert, None, None, dp),
            P(expert, dp, None),
        ),
        out_specs=P(everyone, None),
        check_vma=False,
    )
```

```python
import functools

import jax
import jax.numpy as jnp
from jax import lax
from jax.experimental import pallas as pl
from jax.experimental.pallas import tpu as pltpu
from jax.sharding import Mesh
from jax.sharding import PartitionSpec as P

QH = 64
KVH = 8
HD = 64
E = 32
CAP = 20
TOP = 4
TERMS = 3
BACK = (2, 3, 0, 1)
GROUP = QH // KVH
TILE = 32
VMEM_MIB = 58

norm_eps = 1e-05
F32 = jnp.float32
BF16 = jnp.bfloat16


def params(mib, **kw):
    return pltpu.CompilerParams(vmem_limit_bytes=mib << 20, **kw)


def attend_kernel(
    col_s, rows_s, ctx_s, table_s, sink_s, q_ref, kv_ref, *refs, kv_heads, reqs, per_req
):
    o_ref = refs[-1]
    page_len = kv_ref.shape[1]
    span = per_req * page_len
    width = 2 * HD
    lane = lax.broadcasted_iota(jnp.int32, (1, width), 1)
    low = lane < HD
    slot = lax.broadcasted_iota(jnp.int32, (1, span), 1)
    row_in = lax.broadcasted_iota(jnp.int32, (TILE, 1), 0)
    head0 = col_s[0] * kv_heads * GROUP

    def one_tile(req, first, last, tile):
        r0 = pl.multiple_of(tile * TILE, TILE)
        row = row_in + r0
        mine = (row >= first) & (row < last)
        limit = jnp.where(mine, row + (ctx_s[req] - last), -1)
        limit = jnp.concatenate([limit] * GROUP, axis=0)
        seen = slot <= limit
        for k in range(kv_heads):
            kv = jnp.concatenate(
                [
                    kv_ref[table_s[req * per_req + p], :, k * width : (k + 1) * width]
                    for p in range(per_req)
                ],
                axis=0,
            )
            parts, sinks = [], []
            for g in range(0, GROUP, 2):
                c0 = (k * GROUP + g) * HD
                pair = q_ref[pl.ds(r0, TILE), c0 : c0 + width].astype(F32) * (HD**-0.5)
                parts.append(jnp.where(low, pair, 0.0).astype(BF16))
                parts.append(jnp.where(low, pltpu.roll(pair, HD, 1), 0.0).astype(BF16))
                for h in (g, g + 1):
                    sinks.append(jnp.full((TILE, 1), sink_s[head0 + k * GROUP + h], F32))
            q = jnp.concatenate(parts, axis=0)
            sink = jnp.concatenate(sinks, axis=0)
            score = lax.dot_general(q, kv, (((1,), (1,)), ((), ())), preferred_element_type=F32)
            score = jnp.where(seen, score, -jnp.inf)
            top = jnp.maximum(jnp.max(score, axis=1, keepdims=True), sink)
            prob = jnp.exp(score - top).astype(BF16)
            ones_v = jnp.where(low, jnp.ones_like(kv), kv)
            both = jnp.dot(prob, ones_v, preferred_element_type=F32)
            swapped = pltpu.roll(both, HD, 1)
            norm = jnp.where(low, both, swapped) + jnp.exp(sink - top)
            out = jnp.where(low, swapped, both) / norm
            for g in range(0, GROUP, 2):
                a = out[g * TILE : (g + 1) * TILE]
                b = out[(g + 1) * TILE : (g + 2) * TILE]
                c0 = (k * GROUP + g) * HD
                old = o_ref[pl.ds(r0, TILE), c0 : c0 + width]
                new = jnp.where(low, a, b).astype(BF16)
                o_ref[pl.ds(r0, TILE), c0 : c0 + width] = jnp.where(mine, new, old)

    def one_req(req, first):
        last = first + rows_s[req]

        def step(tile, carry):
            one_tile(req, first, last, tile)
            return carry

        lax.fori_loop(first // TILE, (last - 1) // TILE + 1, step, 0)
        return last

    lax.fori_loop(0, reqs, one_req, jnp.int32(0))


def attend_group(
    col, queries, kv_pages, page_table, new_rows, context, sink_logits, groups, before=()
):
    rows = queries.shape[0]
    pages, page_len, kv_width = kv_pages.shape
    reqs, per_req = page_table.shape
    kv_heads = KVH // groups
    q_width = queries.shape[1] // groups
    body = functools.partial(attend_kernel, kv_heads=kv_heads, reqs=reqs, per_req=per_req)
    flops = 2 * 2 * rows * q_width * per_req * page_len
    return pl.pallas_call(
        body,
        grid_spec=pltpu.PrefetchScalarGridSpec(
            num_scalar_prefetch=5,
            grid=(1,),
            in_specs=[
                pl.BlockSpec((rows, q_width), lambda i, col, *_: (0, col[0])),
                pl.BlockSpec(
                    (pages, page_len, kv_width // groups), lambda i, col, *_: (0, 0, col[0])
                ),
                *[pl.BlockSpec(memory_space=pl.ANY)] * len(before),
            ],
            out_specs=pl.BlockSpec((rows, q_width), lambda i, *_: (0, 0)),
        ),
        out_shape=jax.ShapeDtypeStruct((rows, q_width), BF16),
        compiler_params=params(VMEM_MIB),
        cost_estimate=pl.CostEstimate(
            flops=8 * flops,
            bytes_accessed=2 * (2 * rows * q_width + pages * page_len * kv_width // groups),
            transcendentals=0,
        ),
        name="attend",
    )(col, new_rows, context, page_table.reshape(-1), sink_logits, queries, kv_pages, *before)


def mix_kernel(x_ref, a_ref, b_ref, c_ref, d_ref, gain_ref, info_ref, mixed_ref, normed_ref):
    total = a_ref[...].astype(F32) + b_ref[...].astype(F32)
    total = total + c_ref[...].astype(F32) + d_ref[...].astype(F32)
    mixed = (x_ref[...].astype(F32) + total).astype(BF16)
    mixed_ref[...] = mixed
    m = mixed.astype(F32)
    scale = lax.rsqrt(jnp.mean(m * m, axis=0, keepdims=True) + norm_eps)
    normed = (jnp.transpose(m * scale) * gain_ref[...]).astype(BF16)
    rows, width = normed.shape
    normed_ref[:, :width] = normed
    fill = normed_ref.shape[1] - width
    if fill:
        lane = lax.broadcasted_iota(jnp.int32, (rows, 128), 1) - (128 - fill)
        rest = info_ref[...]
        info = rest.astype(BF16).astype(F32)
        for i in range(1, TERMS):
            rest = rest - rest.astype(BF16).astype(F32)
            moved = pltpu.roll(rest.astype(BF16).astype(F32), i * TOP, 1)
            info = jnp.where((lane >= (i + 1) * TOP) & (lane < (i + 2) * TOP), moved, info)
        normed_ref[:, width:] = info[:, 128 - fill :].astype(BF16)


def mix_and_norm(hidden_t, terms_t, norm_gain, routes, route_weights):
    width, rows = hidden_t.shape
    fill = -width % 128
    info = jnp.concatenate([routes.astype(F32), route_weights], axis=1)
    info = jnp.pad(info, ((0, 0), (128 - fill, fill - info.shape[1]))) if fill else jnp.zeros((rows, 128))
    normed = jax.ShapeDtypeStruct((rows, -(-width // 128) * 128), BF16)
    return pl.pallas_call(
        mix_kernel,
        out_shape=[jax.ShapeDtypeStruct((width, rows), BF16), normed],
        compiler_params=params(VMEM_MIB),
        name="mix_norm",
    )(hidden_t, *terms_t, norm_gain.reshape(1, width), info)


def finish_kernel(mixed_ref, *refs):
    parts, out_ref = refs[:-1], refs[-1]
    total = parts[0][...].astype(F32)
    for part in parts[1:]:
        total = total + part[...].astype(F32)
    total = jnp.transpose(total)[: mixed_ref.shape[0]]
    out_ref[...] = (mixed_ref[...].astype(F32) + total).astype(BF16)


def finish(mixed_t, parts):
    return pl.pallas_call(
        finish_kernel,
        out_shape=jax.ShapeDtypeStruct(mixed_t.shape, BF16),
        compiler_params=params(VMEM_MIB),
        name="finish",
    )(mixed_t, *parts)


def pick_kernel(bases_s, *refs, count, local, width):
    pieces, (x_ref, far_ref, hot_ref) = refs[:count], refs[-3:]
    each, wide = pieces[0].shape
    slots = count * CAP
    both = 2 * local
    at = width - (wide - 128)
    upper = (
        lax.broadcasted_iota(jnp.int32, (each, each), 0)
        <= lax.broadcasted_iota(jnp.int32, (each, each), 1)
    ).astype(F32).astype(BF16)
    members = []
    for s in range(count):
        info = jnp.transpose(pieces[s][:, wide - 128 :].astype(F32))[at : at + TOP]
        for e in range(both):
            expert = (bases_s[e // local] + e % local).astype(F32)
            members.append(jnp.max(jnp.where(info == expert, 1.0, 0.0), axis=0, keepdims=True))
    member = jnp.concatenate(members, axis=0)
    counts = jnp.dot(member.astype(BF16), upper, preferred_element_type=F32)
    rank = jnp.where(member > 0.0, counts - 1.0, -100.0)
    place = lax.broadcasted_iota(jnp.int32, (slots, each), 0).astype(F32)
    columns = []
    for s in range(count):
        want = place - float(s * CAP)
        hots = [
            jnp.where(want == rank[s * both + e : s * both + e + 1], 1.0, 0.0) for e in range(both)
        ]
        columns.append(jnp.concatenate(hots, axis=0).astype(BF16))
    hot = jnp.concatenate(columns, axis=1)
    rows = jnp.concatenate([ref[...] for ref in pieces], axis=0)
    half = local * slots
    for i, ref in enumerate((x_ref, far_ref)):
        picked = jnp.dot(hot[i * half : (i + 1) * half], rows, preferred_element_type=F32)
        ref[...] = picked.astype(BF16).reshape(ref.shape)
    rank_t = jnp.transpose(rank).astype(BF16)
    slot = lax.broadcasted_iota(jnp.int32, (count * both, both * slots), 1)
    line = lax.broadcasted_iota(jnp.int32, (count * both, both * slots), 0)
    for i, s in enumerate(BACK):
        first = (line - s * both) * slots
        owner = (slot >= first) & (slot < first + slots) & (line >= s * both)
        owner = owner & (line < (s + 1) * both)
        owner = jnp.where(owner, 1.0, 0.0)
        want = slot[:1] - s * CAP - jnp.sum(
            jnp.where(owner > 0.0, line - s * both, 0), axis=0, keepdims=True
        ) * slots
        held = jnp.dot(rank_t, owner.astype(BF16), preferred_element_type=F32)
        hot_ref[i * each : (i + 1) * each, :] = jnp.where(held == want.astype(F32), 1.0, 0.0).astype(
            BF16
        )


def pick_rows(bases, pieces, local, width, before=(), later=()):
    count = len(pieces)
    each, wide = pieces[0][0].shape
    slots = count * CAP
    smem = pl.BlockSpec(memory_space=pltpu.SMEM)
    vmem = pl.BlockSpec(memory_space=pltpu.VMEM)
    hand_on = pl.BlockSpec(memory_space=pl.ANY)
    spots = [pl.BlockSpec((each, wide), functools.partial(lambda at, i: (at, 0), at)) for _, at in pieces]
    x = jax.ShapeDtypeStruct((local, slots, wide), BF16)
    return pl.pallas_call(
        functools.partial(pick_kernel, count=count, local=local, width=width),
        grid=(1,),
        in_specs=[smem] + spots + [hand_on] * (len(before) + len(later)),
        out_specs=[hand_on] * len(later) + [vmem] * 3,
        out_shape=[jax.ShapeDtypeStruct(p.shape, p.dtype) for p in later]
        + [x, x, jax.ShapeDtypeStruct((count * each, 2 * local * slots), BF16)],
        input_output_aliases={1 + count + len(before) + i: i for i in range(len(later))},
        compiler_params=params(VMEM_MIB),
        cost_estimate=pl.CostEstimate(
            flops=2 * 4 * local * slots * count * each * wide,
            bytes_accessed=2 * (count * each + 2 * local * slots) * wide,
            transcendentals=0,
        ),
        name="pick",
    )(bases, *[piece for piece, _ in pieces], *before, *later)


def expert_kernel(bases_s, *refs, groups):
    xs, (up_ref, down_ref) = refs[:groups], refs[groups : groups + 2]
    mine_ref, *far_refs = refs[groups + 2 :]
    width = down_ref.shape[1]
    wide = xs[0].shape[2]
    x = jnp.concatenate([ref[0] for ref in xs], axis=0)
    gate = jnp.dot(x[:, :width], up_ref[0, 0], preferred_element_type=F32)
    up = jnp.dot(x[:, :width], up_ref[0, 1], preferred_element_type=F32)
    act = ((up + 1.0) * gate * jax.nn.sigmoid(1.702 * gate)).astype(BF16)
    part = lax.dot_general(
        act, down_ref[0], (((1,), (1,)), ((), ())), preferred_element_type=F32
    )
    info = x[:, wide - 128 :].astype(F32)
    lane = lax.broadcasted_iota(jnp.int32, info.shape, 1) - (width - (wide - 128))
    share = 0.0
    for i in range(TERMS):
        share = share + pltpu.roll(info, 128 - (i + 1) * TOP, 1)
    expert = (bases_s[0] + pl.program_id(0)).astype(F32)
    mine = (lane >= 0) & (lane < TOP) & (info == expert)
    share = jnp.sum(jnp.where(mine, share, 0.0), axis=1, keepdims=True)
    slots = xs[0].shape[1]
    for i in range(groups):
        at = slice(i * slots, (i + 1) * slots)
        y = (part[at] * share[at]).astype(BF16)
        chunk = i // 2
        y_ref, place = (far_refs[chunk], 0) if i % 2 else (mine_ref, chunk)
        to = slice(place * slots, (place + 1) * slots)
        y_ref[0, to, :width] = y
        if wide > width:
            y_ref[0, to, width:] = jnp.zeros((slots, wide - width), BF16)


def run_experts(bases, xs, gate_up, down_t):
    groups = len(xs)
    local, slots, wide = xs[0].shape
    width, units = gate_up.shape[2:]
    heights = [groups // 2 * slots] + [slots] * (groups // 2)
    return pl.pallas_call(
        functools.partial(expert_kernel, groups=groups),
        grid=(local,),
        in_specs=[
            pl.BlockSpec(memory_space=pltpu.SMEM),
            *[pl.BlockSpec((1, slots, wide), lambda e: (e, 0, 0))] * groups,
            pl.BlockSpec((1, 2, width, units), lambda e: (e, 0, 0, 0)),
            pl.BlockSpec((1, width, units), lambda e: (e, 0, 0)),
        ],
        out_specs=[pl.BlockSpec((1, h, wide), lambda e: (e, 0, 0)) for h in heights],
        out_shape=[jax.ShapeDtypeStruct((local, h, wide), BF16) for h in heights],
        compiler_params=params(VMEM_MIB),
        cost_estimate=pl.CostEstimate(
            flops=2 * 2 * 3 * groups * local * slots * width * units,
            bytes_accessed=2 * (gate_up.size + down_t.size + 2 * groups * xs[0].size),
            transcendentals=0,
        ),
        name="experts",
    )(bases, *xs, gate_up, down_t)


def spread_kernel(*refs, count):
    hots, mine_ref, fars = refs[:count], refs[count], refs[count + 1 : 2 * count + 1]
    leave_ref, keep_ref = refs[-2:]
    each = hots[0].shape[0] // len(BACK)
    local, slots, wide = mine_ref.shape
    slots = slots // count
    for c in range(count):
        y = [mine_ref[:, c * slots : (c + 1) * slots, :], fars[c][...]]
        y = jnp.concatenate([part.reshape(local * slots, wide) for part in y], axis=0)
        for i in range(2):
            hot = hots[c][2 * i * each : 2 * (i + 1) * each, :]
            total = jnp.dot(hot, y, preferred_element_type=F32).astype(BF16)
            for j in range(2):
                at = (j * count + c) * each
                ref = (leave_ref, keep_ref)[i]
                ref[at : at + each, :] = total[j * each : (j + 1) * each]


def spread_rows(hots, mine, fars, first):
    count = len(hots)
    rows, depth = hots[0].shape
    local, slots, wide = fars[0].shape
    vmem = pl.BlockSpec(memory_space=pltpu.VMEM)
    return pl.pallas_call(
        functools.partial(spread_kernel, count=count),
        grid=(1,),
        in_specs=[vmem] * count
        + [pl.BlockSpec((local, count * slots, wide), lambda i: (0, first // count, 0))]
        + [vmem] * count,
        out_specs=[vmem] * 2,
        out_shape=[jax.ShapeDtypeStruct((count * rows // 2, wide), BF16)] * 2,
        compiler_params=params(VMEM_MIB),
        cost_estimate=pl.CostEstimate(
            flops=4 * count * rows * depth * wide,
            bytes_accessed=2 * count * (2 * fars[0].size + rows * wide),
            transcendentals=0,
        ),
        name="spread",
    )(*hots, mine, *fars)


def exchange(value, axes, count, step):
    return lax.ppermute(value, axes, [(i, i ^ step) for i in range(count)])


def add(*terms):
    total = terms[0].astype(F32)
    for term in terms[1:]:
        total = total + term.astype(F32)
    return total.astype(BF16)


def together_kernel(*refs):
    pass


def together(*arrays):
    return pl.pallas_call(
        together_kernel,
        in_specs=[pl.BlockSpec(memory_space=pl.ANY)] * len(arrays),
        out_specs=[pl.BlockSpec(memory_space=pl.ANY)] * len(arrays),
        out_shape=[jax.ShapeDtypeStruct(a.shape, a.dtype) for a in arrays],
        input_output_aliases={i: i for i in range(len(arrays))},
        name="together",
    )(*arrays)


def turn_kernel(keep_ref, came_ref, *refs):
    refs[-1][...] = add(keep_ref[...], came_ref[...])


def turn_rows(keep, came, before):
    rows, wide = keep.shape
    half = pl.BlockSpec((rows // 2, wide), lambda i: (1, 0))
    return pl.pallas_call(
        turn_kernel,
        grid=(1,),
        in_specs=[half, half] + [pl.BlockSpec(memory_space=pl.ANY)] * len(before),
        out_specs=pl.BlockSpec((rows // 2, wide), lambda i: (0, 0)),
        out_shape=jax.ShapeDtypeStruct((rows // 2, wide), BF16),
        compiler_params=params(VMEM_MIB),
        name="turn",
    )(keep, came, *before)


def attention_and_norm(
    hidden_in, queries, kv_pages, page_table, new_rows, context, sink_logits, out_proj, norm_gain,
    routes, route_weights, dp, dp_count,
):
    me = lax.axis_index(dp)

    def attend(step, before=()):
        col = (me ^ step).astype(jnp.int32).reshape(1)
        part = attend_group(
            col, queries, kv_pages, page_table, new_rows, context, sink_logits, dp_count, before
        )
        return exchange(part, dp, dp_count, step) if step else part

    def project(part):
        term = jnp.dot(part, out_proj, preferred_element_type=F32).astype(BF16)
        return jnp.swapaxes(term, 0, 1)

    order = list(range(dp_count - 1, 0, -1)) + [0]
    parts, terms, back = [], [], []
    for at, step in enumerate(order):
        before = list(terms[-1:]) if at > 1 else []
        parts.append(attend(step, before))
        if at:
            terms.append(project(parts[at - 1]))
            back.append(exchange(terms[-1], dp, dp_count, order[at - 1]))
    terms = back + [project(parts[-1])]
    hidden_t = jnp.swapaxes(hidden_in, 0, 1)
    return mix_and_norm(hidden_t, terms, norm_gain, routes, route_weights)


def layer_gathered(
    hidden_in, queries, kv_pages, page_table, new_rows, context, sink_logits, out_proj, norm_gain,
    routes, route_weights, gate_up, down_proj, *, sizes,
):
    ny, nx, nz, nc = sizes
    local, _, width, _ = gate_up.shape
    core = lax.axis_index("core")
    bases = (lax.axis_index("z") * nc + jnp.stack([core, core ^ 1])) * local
    bases = bases.astype(jnp.int32)
    everyone = ("y", "x", "z", "core")
    per_y, per_x = nx * nz * nc, nz * nc
    hops = {"first": (per_x, per_y), "second": (per_y, per_x)}

    def to(value, axis, step=1):
        if axis in hops:
            pairs = [(i, i ^ hops[axis][i % nc]) for i in range(ny * nx * nz * nc)]
            return lax.ppermute(value, everyone, pairs)
        return exchange(value, axis, nz if axis == "z" else nc, step)

    mixed, normed = attention_and_norm(
        hidden_in, queries, kv_pages, page_table, new_rows, context, sink_logits, out_proj,
        norm_gain, routes, route_weights, ("y", "x"), ny * nx,
    )
    each = normed.shape[0]
    down_t = jnp.swapaxes(down_proj, 1, 2)
    rows = {0: normed, 1: to(normed, "z", 1), 2: to(normed, "z", 2)}

    def gather(values, both=False):
        one, two = to(values, "first"), to(values, "second")
        if both:
            one, two = together(one, two)
        return values, one, two, to(one, "second")

    def pick(r, arrays, at, **order):
        pieces = [(rows[r], 0)] + [(array, at) for array in arrays[1:]]
        *later, x, far, hot = pick_rows(bases, pieces, local, width, **order)
        return later, [x, to(far, "core")], hot

    def reduce(hots, mine, fars, first):
        count = len(hots)
        half = count * each
        leave, keep = spread_rows(hots, mine, [to(far, "core") for far in fars], first)
        return keep, to(leave, "second"), leave

    def total(keep, came, turn_before=None):
        half = came.shape[0] // 2
        if turn_before is None:
            last = to(add(keep[half:], came[half:]), "first")
        else:
            last = to(turn_rows(keep, came, turn_before), "first")
        parts = [slice(at, at + each) for at in range(0, half, each)]
        return [add(keep[at], came[at], last[at]) for at in parts]

    (rows[1], rows[2]), x_0, hot_0 = pick(0, gather(rows[0]), 0, later=[rows[1], rows[2]])
    rows[3] = to(rows[2], "z", 1)
    (rows[3],), x_2, hot_2 = pick(2, gather(rows[2]), 0, later=[rows[3]])
    mine, *fars = run_experts(bases, x_0 + x_2, gate_up, down_t)
    keep_a, came_a, leave = reduce([hot_0, hot_2], mine, fars, 0)
    plane = gather(jnp.concatenate([rows[3], rows[1]], axis=0), both=True)
    _, x_3, hot_3 = pick(3, plane, 0, before=[leave])
    _, x_1, hot_1 = pick(1, plane, 1, before=[leave])
    mine, *fars = run_experts(bases, x_3 + x_1, gate_up, down_t)
    keep_3, came_3, leave = reduce([hot_3], mine, fars[:1], 0)
    keep_1, came_1, _ = reduce([hot_1], mine, fars[1:], 1)
    sum_0, sum_2 = total(keep_a, came_a, [leave])
    sum_2 = to(sum_2, "z", 2)
    (sum_3,) = total(keep_3, came_3)
    (sum_1,) = total(keep_1, came_1, [sum_2])
    sums = [sum_0, sum_2, to(sum_3, "z", 3), to(sum_1, "z", 1)]
    return jnp.swapaxes(finish(mixed, sums), 0, 1)


def layer_sent(
    hidden_in, queries, kv_pages, page_table, new_rows, context, sink_logits, out_proj, norm_gain,
    routes, route_weights, gate_up, down_proj, *, dp_count,
):
    row_count, model_width = hidden_in.shape
    mixed, normed = attention_and_norm(
        hidden_in, queries, kv_pages, page_table, new_rows, context, sink_logits, out_proj,
        norm_gain, routes, route_weights, "dp", dp_count,
    )
    mixed = jnp.swapaxes(mixed, 0, 1)
    normed = normed[:, :model_width]
    assign = routes.reshape(-1)
    onehot = (assign[:, None] == jnp.arange(E, dtype=jnp.int32)[None, :]).astype(jnp.int32)
    slot_index = jnp.sum((jnp.cumsum(onehot, axis=0) - onehot) * onehot, axis=1)
    source = jnp.arange(assign.shape[0], dtype=jnp.int32) // routes.shape[1]
    send_rows = jnp.zeros((E, CAP, model_width), BF16).at[assign, slot_index].set(normed[source])
    copies = jnp.broadcast_to(send_rows[None], (dp_count,) + send_rows.shape)
    copies = copies.reshape(dp_count * E, CAP, model_width)
    everyone = ("dp", "expert")
    blocks = lax.all_to_all(copies, everyone, split_axis=0, concat_axis=0, tiled=True)
    local = gate_up.shape[0]
    shape = blocks.shape
    blocks = blocks.reshape(shape[0] // local, local, CAP, model_width)
    gate_up_f = jnp.einsum("sjcd,jtdf->sjctf", blocks, gate_up, preferred_element_type=F32)
    gate, up = gate_up_f[:, :, :, 0, :], gate_up_f[:, :, :, 1, :]
    hidden = ((up + 1.0) * gate * jax.nn.sigmoid(1.702 * gate)).astype(BF16)
    partials = jnp.einsum("sjcf,jfd->sjcd", hidden, down_proj, preferred_element_type=F32)
    partials = partials.astype(BF16).reshape(shape)
    back = lax.all_to_all(partials, everyone, split_axis=0, concat_axis=0, tiled=True)
    back = jnp.sum(back.reshape(dp_count, E, CAP, model_width).astype(F32), axis=0)
    picked = back[assign, slot_index] * route_weights.reshape(-1)[:, None]
    mix = jnp.sum(picked.reshape(row_count, routes.shape[1], model_width), axis=1)
    return (mixed.astype(F32) + mix).astype(BF16)


def solution(mesh):
    dp_count, expert_count = mesh.shape["dp"], mesh.shape["expert"]
    if dp_count == 4 and expert_count == 8:
        sizes = (2, 2, 4, 2)
        grid = Mesh(mesh.devices.reshape(sizes), ("y", "x", "z", "core"))
        dp, expert, body = ("y", "x"), ("z", "core"), functools.partial(layer_gathered, sizes=sizes)
    else:
        grid = mesh
        dp, expert, body = ("dp",), ("expert",), functools.partial(layer_sent, dp_count=dp_count)
    everyone = dp + expert
    return jax.shard_map(
        body,
        mesh=grid,
        in_specs=(
            P(everyone, None),
            P(everyone, None),
            P(everyone, None, None),
            P(everyone, None),
            P(everyone),
            P(everyone),
            P(),
            P(dp, None),
            P(),
            P(everyone, None),
            P(everyone, None),
            P(expert, None, None, dp),
            P(expert, dp, None),
        ),
        out_specs=P(everyone, None),
        check_vma=False,
    )
```
